32 devices in a mesh: row: 4 (over x, core), sector: 4 (over z), band: 2 (over y).
Axes of the slice: x: 2, y: 2, z: 4, core: 2. Of those that a mesh axis runs over, the one named last changes fastest.
Arguments:
- residual: float32 [4, 4, 2, 320, 128], P('row', 'sector', 'band'), may hold values from -8 to 8
- block_inverse: float32 [4, 4, 2, 320, 320], P('row', 'sector', 'band'), may hold values from -0.3125 to 0.3125
- cycle_coupling: float32 [4, 4, 320, 320], P('row', 'sector'), as said below
- outlet_flux: float32 [4, 4, 2, 80, 320], P('row', 'sector', 'band'), may hold values from -0.3125 to 0.3125
- inlet_lift: float32 [4, 4, 2, 320, 80], P('row', 'sector', 'band'), may hold values from -0.5 to 0.5
- mortar_shift: int32 [3], replicated, may hold values from 0 to 3
Outputs:
- correction: float32 [4, 4, 2, 320, 128], P('row', 'sector', 'band')
- outlet_traces: float32 [4, 4, 2, 80, 128], P('row', 'sector', 'band')
The draws below stay inside these ranges and needn't reach their ends.
Inputs may be any that keep to these rules, and one draw needn't show every extreme that they name: `mortar_shift`: one sector shift for each of the 3 interfaces between consecutive rows. `cycle_coupling`: each matrix is a positive diagonal plus full off-diagonal entries.
All inputs are finite; a program needn't handle non-finite values.
Results may differ from the reference program's by a relative error of at most 0.00017.
Values sent between devices are 32-bit elements; how exact they have to be, the bound alone decides.
A program may use at most 64 MiB of HBM per device.

```python
import jax
import jax.numpy as jnp
from jax import lax

BLK = 320
FACE = 80
LB = 128
BLADE_ROWS = 4
SECTOR_COUNT = 4
BANDS = 2


def draw_cycle_coupling(key, part):
    random_keys = jax.random.split(jax.random.fold_in(key, 7), 6)
    slow_share = 0.5
    spread = 0.2
    slow_part = jax.random.uniform(random_keys[0], (BLADE_ROWS, SECTOR_COUNT, BLK)) < slow_share
    memory = jax.random.uniform(random_keys[1], (BLADE_ROWS, SECTOR_COUNT, BLK), minval=0.3, maxval=1.5)
    fast = jax.random.uniform(random_keys[2], (BLADE_ROWS, SECTOR_COUNT, BLK), minval=0.2, maxval=0.6)
    decay_rate = jnp.where(slow_part, jnp.exp(-memory / SECTOR_COUNT), fast)
    sudden_jump = jax.random.uniform(random_keys[3], (BLADE_ROWS, SECTOR_COUNT, 1)) < 2.0 / SECTOR_COUNT
    sector_split = jax.random.uniform(random_keys[4], (BLADE_ROWS, SECTOR_COUNT, BLK), minval=0.5, maxval=0.8)
    decay_rate = jnp.where(jnp.logical_and(sudden_jump, slow_part), decay_rate * sector_split, decay_rate)
    off_diag = jax.random.normal(random_keys[5], (BLADE_ROWS, SECTOR_COUNT, BLK, BLK), jnp.float32) * (spread / BLK ** 0.5)
    eye = jnp.eye(BLK, dtype=jnp.float32)
    return off_diag + decay_rate[..., None] * eye


def block_scale(stream_key, shape, cuts, low, top_value):
    loudness = 1.0
    for position, blocks in cuts:
        heights = jax.random.uniform(jax.random.fold_in(jax.random.fold_in(stream_key, 6), position), (blocks,), jnp.float32, low / len(cuts), top_value / len(cuts))
        loudness = loudness * jnp.repeat(jnp.exp(heights), shape[position] // blocks).reshape((-1,) + (1,) * (len(shape) - 1 - position))
    return loudness


def scatter_about(own_key, extent, width, bound, shards=(), kind=jnp.bfloat16):
    values = jax.random.normal(own_key, extent, jnp.float32) * width
    if len(shards) > 0:
        values = block_scale(own_key, extent, shards, -0.22, 0.18) * values
    return jnp.clip(values, min=-bound, max=bound).astype(kind)


def setup_inputs(seed: int = 0) -> dict:
    key_list = jax.random.split(jax.random.key(seed), 7)
    residual = scatter_about(key_list[0], (BLADE_ROWS, SECTOR_COUNT, BANDS, BLK, LB), 1.0, 8.0, ((0, 4), (1, 4), (2, 2)), jnp.float32)
    block_inverse = scatter_about(key_list[1], (BLADE_ROWS, SECTOR_COUNT, BANDS, BLK, BLK), BLK ** -0.5, 0.3125, ((0, 4), (1, 4), (2, 2)), jnp.float32)
    cycle_coupling = draw_cycle_coupling(jax.random.fold_in(key_list[6], 71), 0)
    outlet_flux = scatter_about(key_list[3], (BLADE_ROWS, SECTOR_COUNT, BANDS, FACE, BLK), BLK ** -0.5, 0.3125, ((0, 4), (1, 4), (2, 2)), jnp.float32)
    inlet_lift = scatter_about(key_list[4], (BLADE_ROWS, SECTOR_COUNT, BANDS, BLK, FACE), (2 * FACE) ** -0.5, 0.5, ((0, 4), (1, 4), (2, 2)), jnp.float32)
    mortar_shift = jax.random.randint(key_list[5], (BLADE_ROWS - 1,), 0, SECTOR_COUNT).astype(jnp.int32)
    return dict(residual=residual, block_inverse=block_inverse, cycle_coupling=cycle_coupling, outlet_flux=outlet_flux, inlet_lift=inlet_lift, mortar_shift=mortar_shift)


HIGH = lax.Precision.HIGHEST


def cycle_solve(coupling, source):
    eye = jnp.eye(coupling.shape[1], dtype=jnp.float32)
    zero = jnp.zeros(source.shape[1:], jnp.float32)

    def forward(carry, item):
        matrix, state = carry
        link, term = item
        nxt = (jnp.dot(link, matrix, precision=HIGH),
               term + jnp.einsum('ij,bjl->bil', link, state, precision=HIGH))
        return nxt, carry

    def backward(carry, item):
        matrix, state = carry
        link, term = item
        nxt = (jnp.dot(matrix, link, precision=HIGH),
               state + jnp.einsum('ij,bjl->bil', matrix, term, precision=HIGH))
        return nxt, carry

    _, (pre_mat, pre_state) = lax.scan(forward, (eye, zero), (coupling, source))
    _, (suf_mat, suf_state) = lax.scan(backward, (eye, zero), (coupling, source), reverse=True)
    arrive = pre_state + jnp.einsum('sij,sbjl->sbil', pre_mat, suf_state, precision=HIGH)
    return source + jnp.einsum('sij,sbjl->sbil', coupling, arrive, precision=HIGH)


def reference(residual, block_inverse, cycle_coupling, outlet_flux, inlet_lift, mortar_shift):
    source = jnp.einsum('rsbij,rsbjl->rsbil', block_inverse, residual, precision=HIGH)
    solved = lax.map(lambda pair: cycle_solve(pair[0], pair[1]), (cycle_coupling, source))
    rows_out = [solved[0]]
    for section in range(1, BLADE_ROWS):
        trace = jnp.einsum('sbfj,sbjl->sbfl', outlet_flux[section - 1], rows_out[-1], precision=HIGH)
        moved = jnp.roll(trace, mortar_shift[section - 1], axis=0)
        rows_out.append(solved[section] + jnp.einsum('sbjf,sbfl->sbjl', inlet_lift[section], moved, precision=HIGH))
    correction = jnp.stack(rows_out, axis=0)
    outlet_traces = jnp.einsum('rsbfj,rsbjl->rsbfl', outlet_flux, correction, precision=HIGH)
    return correction, outlet_traces
```

```python
import functools

import jax
import jax.numpy as jnp
from jax import lax
from jax.experimental import pallas as pl
from jax.experimental.pallas import tpu as pltpu
from jax.sharding import PartitionSpec as P

HIGH = lax.Precision.HIGHEST
MESH = pl.DeviceIdType.MESH
F32 = jnp.float32
BF16 = jnp.bfloat16
RING_LIMIT = 8


def split(value):
    top = value.astype(BF16)
    return top, (value - top.astype(F32)).astype(BF16)


def dot(a, b):
    return jnp.dot(a, b, preferred_element_type=F32)


def times(a_top, a_rest, b):
    b_top, b_rest = split(b)
    width = b.shape[1]
    wide = dot(a_top, jnp.concatenate([b_top, b_rest], axis=1))
    return wide[:, :width] + (wide[:, width:] + dot(a_rest, b_top))


def ring_kernel(
    sectors, rows,
    shift_ref, res_hbm, inv_hbm, coup_hbm, flux_hbm, lift_hbm,
    corr_ref, out_ref,
    res, inv, coup, flux, lift, coup2, flux2, lift2, cross2,
    state, landed, trace, arrived,
    load_sem, send_sem, recv_sem, down_send, down_recv,
):
    row = lax.axis_index("row")
    sector = lax.axis_index("sector")
    ahead = lax.rem(sector + 1, sectors)
    behind = lax.rem(sector + sectors - 1, sectors)

    pairs = [(res_hbm, res), (inv_hbm, inv), (coup_hbm, coup), (flux_hbm, flux), (lift_hbm, lift)]
    loads = [
        pltpu.make_async_copy(src, dst, load_sem.at[i]) for i, (src, dst) in enumerate(pairs)
    ]
    for load in loads:
        load.start()

    barrier = pltpu.get_barrier_semaphore()
    pl.semaphore_signal(barrier, inc=1, device_id={"sector": behind}, device_id_type=MESH)

    @pl.when(row > 0)
    def _():
        for k in range(sectors):
            pl.semaphore_signal(
                barrier, inc=1, device_id_type=MESH,
                device_id={"row": row - 1, "sector": lax.rem(sector + k, sectors)},
            )

    loads[0].wait()
    loads[1].wait()
    state[0] = times(*split(inv[...]), res[...])

    @pl.when(row < rows - 1)
    def _():
        pl.semaphore_wait(barrier, sectors + 1)

    @pl.when(row == rows - 1)
    def _():
        pl.semaphore_wait(barrier, 1)

    def prepare():
        loads[2].wait()
        coup2[0], coup2[1] = split(coup[...])
        loads[3].wait()
        flux2[0], flux2[1] = split(flux[...])
        loads[4].wait()
        lift2[0], lift2[1] = split(lift[...])
        cross2[0], cross2[1] = split(times(flux2[0], flux2[1], lift[...]))

    steps = sectors - 1
    for k in range(steps):
        copy = pltpu.make_async_remote_copy(
            src_ref=state.at[k], dst_ref=landed.at[k],
            send_sem=send_sem.at[k], recv_sem=recv_sem.at[k],
            device_id={"sector": ahead}, device_id_type=MESH,
        )
        copy.start()
        if k == 0:
            prepare()
        copy.wait()
        state[k + 1] = state[0] + times(coup2[0], coup2[1], landed[k])

    trace[...] = times(flux2[0], flux2[1], state[steps])

    @pl.when(row == 0)
    def _():
        corr_ref[...] = state[steps]

    def downs():
        return [
            pltpu.make_async_remote_copy(
                src_ref=trace, dst_ref=arrived.at[sector],
                send_sem=down_send.at[k], recv_sem=down_recv.at[sector],
                device_id={"row": row + 1, "sector": lax.rem(sector + k, sectors)},
                device_id_type=MESH,
            )
            for k in range(sectors)
        ]

    @pl.when(row > 0)
    def _():
        for k in range(sectors):
            pltpu.make_async_remote_copy(
                src_ref=trace, dst_ref=arrived.at[k],
                send_sem=down_send.at[0], recv_sem=down_recv.at[k],
                device_id={"row": row - 1, "sector": sector}, device_id_type=MESH,
            ).wait_recv()
        offset = shift_ref[jnp.maximum(row - 1, 0)]
        moved = arrived[lax.rem(sector + sectors - offset, sectors)]
        trace[...] += times(cross2[0], cross2[1], moved)

    @pl.when(row < rows - 1)
    def _():
        for copy in downs():
            copy.start()

    @pl.when(row > 0)
    def _():
        offset = shift_ref[jnp.maximum(row - 1, 0)]
        moved = arrived[lax.rem(sector + sectors - offset, sectors)]
        corr_ref[...] = state[steps] + times(lift2[0], lift2[1], moved)

    out_ref[...] = trace[...]

    @pl.when(row < rows - 1)
    def _():
        for copy in downs():
            copy.wait_send()


def ring_device(residual, block_inverse, cycle_coupling, outlet_flux, inlet_lift, mortar_shift):
    blk, lines = residual.shape[-2:]
    face = outlet_flux.shape[-2]
    sectors = lax.axis_size("sector")
    rows = lax.axis_size("row")
    vmem = pl.BlockSpec(memory_space=pltpu.VMEM)
    hbm = pl.BlockSpec(memory_space=pl.ANY)
    corr, out = pl.pallas_call(
        functools.partial(ring_kernel, sectors, rows),
        out_shape=(
            jax.ShapeDtypeStruct((blk, lines), F32),
            jax.ShapeDtypeStruct((face, lines), F32),
        ),
        in_specs=[pl.BlockSpec(memory_space=pltpu.SMEM)] + [hbm] * 5,
        out_specs=(vmem, vmem),
        scratch_shapes=[
            pltpu.VMEM((blk, lines), F32),
            pltpu.VMEM((blk, blk), F32),
            pltpu.VMEM((blk, blk), F32),
            pltpu.VMEM((face, blk), F32),
            pltpu.VMEM((blk, face), F32),
            pltpu.VMEM((2, blk, blk), BF16),
            pltpu.VMEM((2, face, blk), BF16),
            pltpu.VMEM((2, blk, face), BF16),
            pltpu.VMEM((2, face, face), BF16),
            pltpu.VMEM((sectors, blk, lines), F32),
            pltpu.VMEM((sectors - 1, blk, lines), F32),
            pltpu.VMEM((face, lines), F32),
            pltpu.VMEM((sectors, face, lines), F32),
            pltpu.SemaphoreType.DMA((5,)),
            pltpu.SemaphoreType.DMA((sectors - 1,)),
            pltpu.SemaphoreType.DMA((sectors - 1,)),
            pltpu.SemaphoreType.DMA((sectors,)),
            pltpu.SemaphoreType.DMA((sectors,)),
        ],
        compiler_params=pltpu.CompilerParams(
            collective_id=0, has_side_effects=True, vmem_limit_bytes=24 * 2**20
        ),
        name="ring",
    )(
        mortar_shift,
        residual.reshape(blk, lines),
        block_inverse.reshape(blk, blk),
        cycle_coupling.reshape(blk, blk),
        outlet_flux.reshape(face, blk),
        inlet_lift.reshape(blk, face),
    )
    return corr.reshape(residual.shape), out.reshape(outlet_flux.shape[:-1] + (lines,))


def from_behind(block, axis, distance):
    devices = range(lax.axis_size(axis))
    route = [((i - distance) % len(devices), i) for i in devices]
    return lax.ppermute(block, axis, route)


def from_behind_2(value, axis, steps):
    count = lax.axis_size(axis)
    leading, last = (max(0, -steps), min(count, count - steps))
    return lax.ppermute(value, axis, [(source, source + steps) for source in range(leading, last)])


def apply_block(matrix, state):
    return jnp.einsum("ij,bjl->bil", matrix, state, precision=HIGH)


def turn_sectors(trace, offset, levels):
    for level in range(levels):
        moved = from_behind(trace, "sector", 2**level)
        trace = jnp.where(offset // 2**level % 2 == 1, moved, trace)
    return trace


def pass_down(trace):
    return from_behind_2(trace, "row", 1)


def doubling_device(residual, block_inverse, cycle_coupling, outlet_flux, inlet_lift, mortar_shift):
    res_local = residual[0, 0]
    inverse = block_inverse[0, 0]
    coupling = cycle_coupling[0, 0]
    flux = outlet_flux[0, 0]
    lift = inlet_lift[0, 0]
    source = jnp.einsum("bij,bjl->bil", inverse, res_local, precision=HIGH)
    levels = lax.axis_size("sector").bit_length() - 1
    matrix = coupling
    state = source
    for level in range(levels):
        if level + 1 < levels:
            prev_matrix, prev_state = from_behind((matrix, state), "sector", 2**level)
            state = state + apply_block(matrix, prev_state)
            matrix = jnp.dot(matrix, prev_matrix, precision=HIGH)
        else:
            prev_state = from_behind(state, "sector", 2**level)
            state = state + apply_block(matrix, prev_state)
    row_count = lax.axis_size("row")
    row_index = lax.axis_index("row")
    offset = jnp.sum(
        jnp.where(jnp.arange(row_count - 1, dtype=jnp.int32) == row_index - 1, mortar_shift, 0)
    )
    bands = state.shape[0]
    current = state
    band_ids = jnp.arange(bands, dtype=jnp.int32)
    for step in range(1, row_count + bands - 1):
        send_band = jnp.clip(step - 1 - row_index, 0, bands - 1)
        flux_one = lax.dynamic_index_in_dim(flux, send_band, 0, keepdims=False)
        state_one = lax.dynamic_index_in_dim(current, send_band, 0, keepdims=False)
        trace = jnp.dot(flux_one, state_one, precision=HIGH)[None]
        moved = turn_sectors(pass_down(trace), offset, levels)[0]
        band = step - row_index
        band_clip = jnp.clip(band, 0, bands - 1)
        lift_one = lax.dynamic_index_in_dim(lift, band_clip, 0, keepdims=False)
        solved_one = lax.dynamic_index_in_dim(state, band_clip, 0, keepdims=False)
        update = solved_one + jnp.dot(lift_one, moved, precision=HIGH)
        valid = jnp.logical_and(row_index >= 1, jnp.logical_and(band >= 0, band < bands))
        chosen = jnp.logical_and(valid, band_ids == band)[:, None, None]
        current = jnp.where(chosen, update[None], current)
    outlet = jnp.einsum("bfj,bjl->bfl", flux, current, precision=HIGH)
    return (current[None, None], outlet[None, None])


def solution(mesh):
    in_specs = (
        P("row", "sector", "band", None, None),
        P("row", "sector", "band", None, None),
        P("row", "sector", None, None),
        P("row", "sector", "band", None, None),
        P("row", "sector", "band", None, None),
        P(),
    )
    out_specs = (P("row", "sector", "band", None, None), P("row", "sector", "band", None, None))
    on_device = ring_device if mesh.shape["sector"] <= RING_LIMIT else doubling_device
    return jax.shard_map(
        on_device, mesh=mesh, in_specs=in_specs, out_specs=out_specs, check_vma=False
    )
```

```python
import functools

import jax
import jax.numpy as jnp
from jax import lax
from jax.experimental import pallas as pl
from jax.experimental.pallas import tpu as pltpu
from jax.sharding import PartitionSpec as P

HIGH = lax.Precision.HIGHEST
MESH = pl.DeviceIdType.MESH
F32 = jnp.float32
BF16 = jnp.bfloat16
RING_LIMIT = 8


def split(value):
    top = value.astype(BF16)
    return top, (value - top.astype(F32)).astype(BF16)


def dot(a, b):
    return jnp.dot(a, b, preferred_element_type=F32)


def times(a_top, a_rest, b):
    b_top, b_rest = split(b)
    width = b.shape[1]
    wide = dot(a_top, jnp.concatenate([b_top, b_rest], axis=1))
    return wide[:, :width] + (wide[:, width:] + dot(a_rest, b_top))


def exchange(value):
    return pltpu.roll(value, value.shape[1] // 2, axis=1)


def pick(left, right):
    lane = lax.broadcasted_iota(jnp.int32, left.shape, 1)
    return jnp.where(lane < left.shape[1] // 2, left, right)


def pack(value):
    half = value.shape[0] // 2
    upper, lower = value[:half], value[half:]
    return pick(upper, exchange(lower)), pick(exchange(upper), lower)


def unpack(first, second):
    return pick(first, exchange(second)), pick(exchange(first), second)


def times_packed(matrix, y):
    half = y.shape[0]
    p = times(matrix[0], matrix[1], y)
    q = times(matrix[2], matrix[3], y)
    return pick(p[:half], q[half:]) + exchange(pick(p[half:], q[:half]))


def ring_kernel(
    sectors, rows,
    shift_ref, res_hbm, inv_hbm, coup_hbm, flux_hbm, lift_hbm,
    corr_ref, out_ref,
    res, inv, coup, flux, lift, coup4, flux2, lift2, cross2,
    state, landed, solved, trace, arrived,
    load_sem, send_sem, recv_sem, down_send, down_recv,
):
    row = lax.axis_index("row")
    sector = lax.axis_index("sector")
    ahead = lax.rem(sector + 1, sectors)
    behind = lax.rem(sector + sectors - 1, sectors)

    pairs = [(res_hbm, res), (inv_hbm, inv), (coup_hbm, coup), (flux_hbm, flux), (lift_hbm, lift)]
    loads = [
        pltpu.make_async_copy(src, dst, load_sem.at[i]) for i, (src, dst) in enumerate(pairs)
    ]
    for load in loads:
        load.start()

    barrier = pltpu.get_barrier_semaphore()
    pl.semaphore_signal(barrier, inc=1, device_id={"sector": behind}, device_id_type=MESH)

    @pl.when(row > 0)
    def _():
        for k in range(sectors):
            pl.semaphore_signal(
                barrier, inc=1, device_id_type=MESH,
                device_id={"row": row - 1, "sector": lax.rem(sector + k, sectors)},
            )

    loads[0].wait()
    loads[1].wait()
    state[0, 0], state[0, 1] = pack(times(*split(inv[...]), res[...]))

    @pl.when(row < rows - 1)
    def _():
        pl.semaphore_wait(barrier, sectors + 1)

    @pl.when(row == rows - 1)
    def _():
        pl.semaphore_wait(barrier, 1)

    steps = sectors - 1

    def ring_copy(k, h):
        return pltpu.make_async_remote_copy(
            src_ref=state.at[k, h], dst_ref=landed.at[k, h],
            send_sem=send_sem.at[k, h], recv_sem=recv_sem.at[k, h],
            device_id={"sector": ahead}, device_id_type=MESH,
        )

    ring_copy(0, 0).start()
    ring_copy(0, 1).start()

    half = coup.shape[1] // 2
    loads[2].wait()
    coup4[0], coup4[1] = split(coup[:, :half])
    coup4[2], coup4[3] = split(coup[:, half:])
    loads[3].wait()
    flux2[0], flux2[1] = split(flux[...])
    loads[4].wait()
    lift_here = lift[...].T
    lift2[0], lift2[1] = split(lift_here)
    cross2[0], cross2[1] = split(times(flux2[0], flux2[1], lift_here))

    for k in range(steps):
        for h in range(2):
            ring_copy(k, h).wait_recv()
            state[k + 1, h] = state[0, h] + times_packed(coup4, landed[k, h])
            if k + 1 < steps:
                ring_copy(k + 1, h).start()

    upper, lower = unpack(state[steps, 0], state[steps, 1])
    solved[:half] = upper
    solved[half:] = lower
    trace[...] = times(flux2[0], flux2[1], solved[...])

    @pl.when(row == 0)
    def _():
        corr_ref[...] = solved[...]

    def downs():
        return [
            pltpu.make_async_remote_copy(
                src_ref=trace, dst_ref=arrived.at[sector],
                send_sem=down_send.at[k], recv_sem=down_recv.at[sector],
                device_id={"row": row + 1, "sector": lax.rem(sector + k, sectors)},
                device_id_type=MESH,
            )
            for k in range(sectors)
        ]

    @pl.when(row > 0)
    def _():
        for k in range(sectors):
            pltpu.make_async_remote_copy(
                src_ref=trace, dst_ref=arrived.at[k],
                send_sem=down_send.at[0], recv_sem=down_recv.at[k],
                device_id={"row": row - 1, "sector": sector}, device_id_type=MESH,
            ).wait_recv()
        offset = shift_ref[jnp.maximum(row - 1, 0)]
        moved = arrived[lax.rem(sector + sectors - offset, sectors)]
        trace[...] += times(cross2[0], cross2[1], moved)

    @pl.when(row < rows - 1)
    def _():
        for copy in downs():
            copy.start()

    @pl.when(row > 0)
    def _():
        offset = shift_ref[jnp.maximum(row - 1, 0)]
        moved = arrived[lax.rem(sector + sectors - offset, sectors)]
        corr_ref[...] = solved[...] + times(lift2[0], lift2[1], moved)

    out_ref[...] = trace[...]

    for k in range(steps):
        for h in range(2):
            ring_copy(k, h).wait_send()

    @pl.when(row < rows - 1)
    def _():
        for copy in downs():
            copy.wait_send()


def ring_device(residual, block_inverse, cycle_coupling, outlet_flux, inlet_lift, mortar_shift):
    blk, lines = residual.shape[-2:]
    face = outlet_flux.shape[-2]
    sectors = lax.axis_size("sector")
    rows = lax.axis_size("row")
    vmem = pl.BlockSpec(memory_space=pltpu.VMEM)
    hbm = pl.BlockSpec(memory_space=pl.ANY)
    corr, out = pl.pallas_call(
        functools.partial(ring_kernel, sectors, rows),
        out_shape=(
            pltpu.VMEM((blk, lines), F32),
            pltpu.VMEM((face, lines), F32),
        ),
        in_specs=[pl.BlockSpec(memory_space=pltpu.SMEM)] + [hbm] * 5,
        out_specs=(vmem, vmem),
        scratch_shapes=[
            pltpu.VMEM((blk, lines), F32),
            pltpu.VMEM((blk, blk), F32),
            pltpu.VMEM((blk, blk), F32),
            pltpu.VMEM((face, blk), F32),
            pltpu.VMEM((face, blk), F32),
            pltpu.VMEM((4, blk, blk // 2), BF16),
            pltpu.VMEM((2, face, blk), BF16),
            pltpu.VMEM((2, blk, face), BF16),
            pltpu.VMEM((2, face, face), BF16),
            pltpu.VMEM((sectors, 2, blk // 2, lines), F32),
            pltpu.VMEM((sectors - 1, 2, blk // 2, lines), F32),
            pltpu.VMEM((blk, lines), F32),
            pltpu.VMEM((face, lines), F32),
            pltpu.VMEM((sectors, face, lines), F32),
            pltpu.SemaphoreType.DMA((5,)),
            pltpu.SemaphoreType.DMA((sectors - 1, 2)),
            pltpu.SemaphoreType.DMA((sectors - 1, 2)),
            pltpu.SemaphoreType.DMA((sectors,)),
            pltpu.SemaphoreType.DMA((sectors,)),
        ],
        compiler_params=pltpu.CompilerParams(
            collective_id=0, has_side_effects=True, vmem_limit_bytes=62 * 2**20
        ),
        name="ring",
    )(
        mortar_shift,
        residual.reshape(blk, lines),
        block_inverse.reshape(blk, blk),
        cycle_coupling.reshape(blk, blk),
        outlet_flux.reshape(face, blk),
        jnp.swapaxes(inlet_lift, -1, -2).reshape(face, blk),
    )
    return corr.reshape(residual.shape), out.reshape(outlet_flux.shape[:-1] + (lines,))


def from_behind(block, axis, distance):
    devices = range(lax.axis_size(axis))
    route = [((i - distance) % len(devices), i) for i in devices]
    return lax.ppermute(block, axis, route)


def from_behind_2(value, axis, steps):
    count = lax.axis_size(axis)
    leading, last = (max(0, -steps), min(count, count - steps))
    return lax.ppermute(value, axis, [(source, source + steps) for source in range(leading, last)])


def apply_block(matrix, state):
    return jnp.einsum("ij,bjl->bil", matrix, state, precision=HIGH)


def turn_sectors(trace, offset, levels):
    for level in range(levels):
        moved = from_behind(trace, "sector", 2**level)
        trace = jnp.where(offset // 2**level % 2 == 1, moved, trace)
    return trace


def pass_down(trace):
    return from_behind_2(trace, "row", 1)


def doubling_device(residual, block_inverse, cycle_coupling, outlet_flux, inlet_lift, mortar_shift):
    res_local = residual[0, 0]
    inverse = block_inverse[0, 0]
    coupling = cycle_coupling[0, 0]
    flux = outlet_flux[0, 0]
    lift = inlet_lift[0, 0]
    source = jnp.einsum("bij,bjl->bil", inverse, res_local, precision=HIGH)
    levels = lax.axis_size("sector").bit_length() - 1
    matrix = coupling
    state = source
    for level in range(levels):
        if level + 1 < levels:
            prev_matrix, prev_state = from_behind((matrix, state), "sector", 2**level)
            state = state + apply_block(matrix, prev_state)
            matrix = jnp.dot(matrix, prev_matrix, precision=HIGH)
        else:
            prev_state = from_behind(state, "sector", 2**level)
            state = state + apply_block(matrix, prev_state)
    row_count = lax.axis_size("row")
    row_index = lax.axis_index("row")
    offset = jnp.sum(
        jnp.where(jnp.arange(row_count - 1, dtype=jnp.int32) == row_index - 1, mortar_shift, 0)
    )
    bands = state.shape[0]
    current = state
    band_ids = jnp.arange(bands, dtype=jnp.int32)
    for step in range(1, row_count + bands - 1):
        send_band = jnp.clip(step - 1 - row_index, 0, bands - 1)
        flux_one = lax.dynamic_index_in_dim(flux, send_band, 0, keepdims=False)
        state_one = lax.dynamic_index_in_dim(current, send_band, 0, keepdims=False)
        trace = jnp.dot(flux_one, state_one, precision=HIGH)[None]
        moved = turn_sectors(pass_down(trace), offset, levels)[0]
        band = step - row_index
        band_clip = jnp.clip(band, 0, bands - 1)
        lift_one = lax.dynamic_index_in_dim(lift, band_clip, 0, keepdims=False)
        solved_one = lax.dynamic_index_in_dim(state, band_clip, 0, keepdims=False)
        update = solved_one + jnp.dot(lift_one, moved, precision=HIGH)
        valid = jnp.logical_and(row_index >= 1, jnp.logical_and(band >= 0, band < bands))
        chosen = jnp.logical_and(valid, band_ids == band)[:, None, None]
        current = jnp.where(chosen, update[None], current)
    outlet = jnp.einsum("bfj,bjl->bfl", flux, current, precision=HIGH)
    return (current[None, None], outlet[None, None])


def solution(mesh):
    in_specs = (
        P("row", "sector", "band", None, None),
        P("row", "sector", "band", None, None),
        P("row", "sector", None, None),
        P("row", "sector", "band", None, None),
        P("row", "sector", "band", None, None),
        P(),
    )
    out_specs = (P("row", "sector", "band", None, None), P("row", "sector", "band", None, None))
    on_device = ring_device if mesh.shape["sector"] <= RING_LIMIT else doubling_device
    return jax.shard_map(
        on_device, mesh=mesh, in_specs=in_specs, out_specs=out_specs, check_vma=False
    )
```

```python
import functools

import jax
import jax.numpy as jnp
from jax import lax
from jax.experimental import pallas as pl
from jax.experimental.pallas import tpu as pltpu
from jax.sharding import PartitionSpec as P

HIGH = lax.Precision.HIGHEST
MESH = pl.DeviceIdType.MESH
F32 = jnp.float32
BF16 = jnp.bfloat16
RING_LIMIT = 8


def split(value):
    top = value.astype(BF16)
    return top, (value - top.astype(F32)).astype(BF16)


def dot(a, b):
    return jnp.dot(a, b, preferred_element_type=F32)


def times(a_top, a_rest, b):
    b_top, b_rest = split(b)
    width = b.shape[1]
    wide = dot(a_top, jnp.concatenate([b_top, b_rest], axis=1))
    return wide[:, :width] + (wide[:, width:] + dot(a_rest, b_top))


def exchange(value):
    return pltpu.roll(value, value.shape[1] // 2, axis=1)


def pick(left, right):
    lane = lax.broadcasted_iota(jnp.int32, left.shape, 1)
    return jnp.where(lane < left.shape[1] // 2, left, right)


def pack(value):
    half = value.shape[0] // 2
    upper, lower = value[:half], value[half:]
    return pick(upper, exchange(lower)), pick(exchange(upper), lower)


def unpack(first, second):
    return pick(first, exchange(second)), pick(exchange(first), second)


def times_packed(matrix, y):
    half = matrix[0].shape[0] // 2
    p = times(matrix[0], matrix[1], y)
    q = times(matrix[2], matrix[3], y)
    return pick(p[:half], q[half:]) + exchange(pick(p[half:], q[:half]))


def columns(matrix):
    half = matrix.shape[1] // 2
    return split(matrix[:, :half]) + split(matrix[:, half:])


def keep(ref, matrix):
    for i, part in enumerate(columns(matrix)):
        ref[i] = part


def ring_kernel(
    sectors,
    shift_ref, res_hbm, inv_hbm, coup_hbm, flux_hbm, lift_hbm,
    corr_ref, out_ref,
    res, inv, coup, flux, lift, coup4, flux4, lift4, cross4, other4,
    state, landed, trace, final, above_a, above_b, beside_a, beside_b, crosses, stage, given,
    load_sem, send_sem, recv_sem, above_recv, beside_recv, trace_send,
    cross_send, cross_recv, stage_send, given_recv,
):
    row = lax.axis_index("row")
    sector = lax.axis_index("sector")
    above, beside = (above_a, above_b), (beside_a, beside_b)

    def turn(k):
        return lax.rem(sector + k, sectors)

    def remote(src, dst, send, recv, down, k):
        return pltpu.make_async_remote_copy(
            src_ref=src, dst_ref=dst, send_sem=send, recv_sem=recv,
            device_id={"row": row + down, "sector": turn(k)}, device_id_type=MESH,
        )

    pairs = [(res_hbm, res), (inv_hbm, inv), (flux_hbm, flux), (lift_hbm, lift), (coup_hbm, coup)]
    loads = [
        pltpu.make_async_copy(src, dst, load_sem.at[i]) for i, (src, dst) in enumerate(pairs)
    ]
    for load in loads:
        load.start()

    barrier = pltpu.get_barrier_semaphore()

    def greet(up, k):
        pl.semaphore_signal(
            barrier, inc=1, device_id={"row": row - up, "sector": turn(k)}, device_id_type=MESH
        )

    greet(0, sectors - 1)

    @pl.when(row == 1)
    def _():
        for k in range(1, sectors - 1):
            greet(0, k)

    @pl.when(row % 2 == 1)
    def _():
        for k in range(sectors):
            greet(1, k)

    @pl.when(row >= 2)
    def _():
        greet(row - 1, 0)

    loads[0].wait()
    loads[1].wait()
    state[0, 0], state[0, 1] = pack(times(*split(inv[...]), res[...]))

    @pl.when(row % 2 == 0)
    def _():
        pl.semaphore_wait(barrier, sectors + 1)

    @pl.when(row == 1)
    def _():
        pl.semaphore_wait(barrier, sectors + 1)

    @pl.when(row == 3)
    def _():
        pl.semaphore_wait(barrier, 1)

    steps = sectors - 1

    def ring_copy(k, h):
        return remote(
            state.at[k, h], landed.at[k, h], send_sem.at[k, h], recv_sem.at[k, h], 0, 1
        )

    ring_copy(0, 0).start()
    ring_copy(0, 1).start()

    loads[2].wait()
    loads[3].wait()
    lift_here = lift[...].T
    cross = times(*split(flux[...]), lift_here)
    crosses[sector] = cross

    def cross_copies():
        return (
            lambda: [
                remote(crosses.at[sector], crosses.at[sector], cross_send.at[k], cross_recv.at[sector], 0, k)
                for k in range(1, sectors)
            ],
            lambda: [
                remote(crosses.at[sector], above_cross(sector), cross_send.at[k], cross_recv.at[sector], 1, k)
                for k in range(sectors)
            ],
        )

    def above_cross(k):
        return crosses.at[sectors + k]

    @pl.when(row == 1)
    def _():
        for copy in cross_copies()[0]():
            copy.start()

    @pl.when(row == 2)
    def _():
        for copy in cross_copies()[1]():
            copy.start()

    keep(flux4, flux[...])
    keep(lift4, lift_here)
    keep(cross4, cross)
    loads[4].wait()
    keep(coup4, coup[...])

    def halves(ref):
        return [ref[i] for i in range(4)]

    shift = [shift_ref[i] for i in range(3)]

    def back(by):
        return lax.rem(sector + 2 * sectors - by, sectors)

    def trace_copies(h):
        return (
            lambda: [
                remote(trace.at[h], above[h].at[sector], trace_send.at[h, k], above_recv.at[h, sector], 1, k)
                for k in range(sectors)
            ],
            lambda: [
                remote(trace.at[h], beside[h].at[sector], trace_send.at[h, k], beside_recv.at[h, sector], 0, k)
                for k in range(1, sectors)
            ],
        )

    for k in range(steps):
        for h in range(2):
            ring_copy(k, h).wait_recv()
            state[k + 1, h] = state[0, h] + times_packed(halves(coup4), landed[k, h])
            if k + 1 < steps:
                ring_copy(k + 1, h).start()
                continue
            trace[h] = times_packed(halves(flux4), state[steps, h])

            @pl.when(row % 2 == 0)
            def _():
                for copy in trace_copies(h)[0]():
                    copy.start()

            @pl.when(row == 1)
            def _():
                for copy in trace_copies(h)[1]():
                    copy.start()

        if k == 0:

            @pl.when(row == 1)
            def _():
                for i in range(1, sectors):
                    remote(
                        crosses.at[turn(i)], crosses.at[turn(i)], cross_send.at[i],
                        cross_recv.at[turn(i)], 0, i,
                    ).wait_recv()
                keep(other4.at[0], crosses[back(shift[1])])
                keep(other4.at[1], crosses[back(shift[1] + shift[2])])

            @pl.when(row == 3)
            def _():
                for i in range(sectors):
                    remote(
                        crosses.at[0], above_cross(i), cross_send.at[i], cross_recv.at[i], -1, i
                    ).wait_recv()
                keep(other4.at[0], crosses[sectors + back(shift[2])])

    def wait_above(h):
        for i in range(sectors):
            remote(
                trace.at[h], above[h].at[i], trace_send.at[h, 0], above_recv.at[h, i], -1, i
            ).wait_recv()

    def stage_copy(h, i):
        return remote(
            stage.at[h, i], given.at[h], stage_send.at[h, i], given_recv.at[h], i + 1, 0
        )

    def finish(h, moved):
        final[h] = trace[h] + times_packed(halves(cross4), moved)
        state[steps, h] += times_packed(halves(lift4), moved)

    @pl.when(row == 0)
    def _():
        final[...] = trace[...]

    @pl.when(row == 1)
    def _():
        for h in range(2):
            wait_above(h)
            for i in range(1, sectors):
                remote(
                    trace.at[h], beside[h].at[turn(i)], trace_send.at[h, i],
                    beside_recv.at[h, turn(i)], 0, i,
                ).wait_recv()
            beside[h][sector] = trace[h]
            for i, by in enumerate((shift[1], shift[1] + shift[2])):
                moved = above[h][lax.rem(back(by) + sectors - shift[0], sectors)]
                stage[h, i] = beside[h][back(by)] + times_packed(halves(other4.at[i]), moved)
                stage_copy(h, i).start()
        for h in range(2):
            finish(h, above[h][back(shift[0])])

    @pl.when(row == 2)
    def _():
        for h in range(2):
            stage_copy(h, 0).wait_recv()
            finish(h, given[h])

    @pl.when(row == 3)
    def _():
        for h in range(2):
            wait_above(h)
            stage_copy(h, 1).wait_recv()
            moved = above[h][back(shift[2])] + times_packed(halves(other4.at[0]), given[h])
            finish(h, moved)

    for ref, first, second in (
        (corr_ref, state[steps, 0], state[steps, 1]), (out_ref, final[0], final[1]),
    ):
        half = first.shape[0]
        ref[:half], ref[half:] = unpack(first, second)

    for k in range(steps):
        for h in range(2):
            ring_copy(k, h).wait_send()

    @pl.when(row % 2 == 0)
    def _():
        for h in range(2):
            for copy in trace_copies(h)[0]():
                copy.wait_send()

    @pl.when(row == 1)
    def _():
        for copy in cross_copies()[0]():
            copy.wait_send()
        for h in range(2):
            for copy in trace_copies(h)[1]():
                copy.wait_send()
            for i in range(2):
                stage_copy(h, i).wait_send()

    @pl.when(row == 2)
    def _():
        for copy in cross_copies()[1]():
            copy.wait_send()


def ring_device(residual, block_inverse, cycle_coupling, outlet_flux, inlet_lift, mortar_shift):
    blk, lines = residual.shape[-2:]
    face = outlet_flux.shape[-2]
    sectors = lax.axis_size("sector")
    steps = sectors - 1
    vmem = pl.BlockSpec(memory_space=pltpu.VMEM)
    hbm = pl.BlockSpec(memory_space=pl.ANY)
    dma = pltpu.SemaphoreType.DMA
    corr, out = pl.pallas_call(
        functools.partial(ring_kernel, sectors),
        out_shape=(pltpu.VMEM((blk, lines), F32), pltpu.VMEM((face, lines), F32)),
        in_specs=[pl.BlockSpec(memory_space=pltpu.SMEM)] + [hbm] * 5,
        out_specs=(vmem, vmem),
        scratch_shapes=[
            pltpu.VMEM((blk, lines), F32),
            pltpu.VMEM((blk, blk), F32),
            pltpu.VMEM((blk, blk), F32),
            pltpu.VMEM((face, blk), F32),
            pltpu.VMEM((face, blk), F32),
            pltpu.VMEM((4, blk, blk // 2), BF16),
            pltpu.VMEM((4, face, blk // 2), BF16),
            pltpu.VMEM((4, blk, face // 2), BF16),
            pltpu.VMEM((4, face, face // 2), BF16),
            pltpu.VMEM((2, 4, face, face // 2), BF16),
            pltpu.VMEM((sectors, 2, blk // 2, lines), F32),
            pltpu.VMEM((steps, 2, blk // 2, lines), F32),
            pltpu.VMEM((2, face // 2, lines), F32),
            pltpu.VMEM((2, face // 2, lines), F32),
            pltpu.VMEM((sectors, face // 2, lines), F32),
            pltpu.VMEM((sectors, face // 2, lines), F32),
            pltpu.VMEM((sectors, face // 2, lines), F32),
            pltpu.VMEM((sectors, face // 2, lines), F32),
            pltpu.VMEM((2 * sectors, face, face), F32),
            pltpu.VMEM((2, 2, face // 2, lines), F32),
            pltpu.VMEM((2, face // 2, lines), F32),
            dma((5,)),
            dma((steps, 2)),
            dma((steps, 2)),
            dma((2, sectors)),
            dma((2, sectors)),
            dma((2, sectors)),
            dma((sectors,)),
            dma((sectors,)),
            dma((2, 2)),
            dma((2,)),
        ],
        compiler_params=pltpu.CompilerParams(
            collective_id=0, has_side_effects=True, vmem_limit_bytes=62 * 2**20
        ),
        name="ring",
    )(
        mortar_shift,
        residual.reshape(blk, lines),
        block_inverse.reshape(blk, blk),
        cycle_coupling.reshape(blk, blk),
        outlet_flux.reshape(face, blk),
        jnp.swapaxes(inlet_lift, -1, -2).reshape(face, blk),
    )
    return corr.reshape(residual.shape), out.reshape(outlet_flux.shape[:-1] + (lines,))


def from_behind(block, axis, distance):
    devices = range(lax.axis_size(axis))
    route = [((i - distance) % len(devices), i) for i in devices]
    return lax.ppermute(block, axis, route)


def from_behind_2(value, axis, steps):
    count = lax.axis_size(axis)
    leading, last = (max(0, -steps), min(count, count - steps))
    return lax.ppermute(value, axis, [(source, source + steps) for source in range(leading, last)])


def apply_block(matrix, state):
    return jnp.einsum("ij,bjl->bil", matrix, state, precision=HIGH)


def turn_sectors(trace, offset, levels):
    for level in range(levels):
        moved = from_behind(trace, "sector", 2**level)
        trace = jnp.where(offset // 2**level % 2 == 1, moved, trace)
    return trace


def pass_down(trace):
    return from_behind_2(trace, "row", 1)


def doubling_device(residual, block_inverse, cycle_coupling, outlet_flux, inlet_lift, mortar_shift):
    res_local = residual[0, 0]
    inverse = block_inverse[0, 0]
    coupling = cycle_coupling[0, 0]
    flux = outlet_flux[0, 0]
    lift = inlet_lift[0, 0]
    source = jnp.einsum("bij,bjl->bil", inverse, res_local, precision=HIGH)
    levels = lax.axis_size("sector").bit_length() - 1
    matrix = coupling
    state = source
    for level in range(levels):
        if level + 1 < levels:
            prev_matrix, prev_state = from_behind((matrix, state), "sector", 2**level)
            state = state + apply_block(matrix, prev_state)
            matrix = jnp.dot(matrix, prev_matrix, precision=HIGH)
        else:
            prev_state = from_behind(state, "sector", 2**level)
            state = state + apply_block(matrix, prev_state)
    row_count = lax.axis_size("row")
    row_index = lax.axis_index("row")
    offset = jnp.sum(
        jnp.where(jnp.arange(row_count - 1, dtype=jnp.int32) == row_index - 1, mortar_shift, 0)
    )
    bands = state.shape[0]
    current = state
    band_ids = jnp.arange(bands, dtype=jnp.int32)
    for step in range(1, row_count + bands - 1):
        send_band = jnp.clip(step - 1 - row_index, 0, bands - 1)
        flux_one = lax.dynamic_index_in_dim(flux, send_band, 0, keepdims=False)
        state_one = lax.dynamic_index_in_dim(current, send_band, 0, keepdims=False)
        trace = jnp.dot(flux_one, state_one, precision=HIGH)[None]
        moved = turn_sectors(pass_down(trace), offset, levels)[0]
        band = step - row_index
        band_clip = jnp.clip(band, 0, bands - 1)
        lift_one = lax.dynamic_index_in_dim(lift, band_clip, 0, keepdims=False)
        solved_one = lax.dynamic_index_in_dim(state, band_clip, 0, keepdims=False)
        update = solved_one + jnp.dot(lift_one, moved, precision=HIGH)
        valid = jnp.logical_and(row_index >= 1, jnp.logical_and(band >= 0, band < bands))
        chosen = jnp.logical_and(valid, band_ids == band)[:, None, None]
        current = jnp.where(chosen, update[None], current)
    outlet = jnp.einsum("bfj,bjl->bfl", flux, current, precision=HIGH)
    return (current[None, None], outlet[None, None])


def solution(mesh):
    in_specs = (
        P("row", "sector", "band", None, None),
        P("row", "sector", "band", None, None),
        P("row", "sector", None, None),
        P("row", "sector", "band", None, None),
        P("row", "sector", "band", None, None),
        P(),
    )
    out_specs = (P("row", "sector", "band", None, None), P("row", "sector", "band", None, None))
    short = mesh.shape["sector"] <= RING_LIMIT and mesh.shape["row"] == 4
    on_device = ring_device if short else doubling_device
    return jax.shard_map(
        on_device, mesh=mesh, in_specs=in_specs, out_specs=out_specs, check_vma=False
    )
```

```python
import functools

import jax
import jax.numpy as jnp
from jax import lax
from jax.experimental import pallas as pl
from jax.experimental.pallas import tpu as pltpu
from jax.sharding import PartitionSpec as P

HIGH = lax.Precision.HIGHEST
MESH = pl.DeviceIdType.MESH
F32 = jnp.float32
BF16 = jnp.bfloat16
RING_LIMIT = 8


def split(value):
    top = value.astype(BF16)
    return top, (value - top.astype(F32)).astype(BF16)


def dot(a, b):
    return jnp.dot(a, b, preferred_element_type=F32)


def times(a_top, a_rest, b):
    b_top, b_rest = split(b)
    width = b.shape[1]
    wide = dot(a_top, jnp.concatenate([b_top, b_rest], axis=1))
    return wide[:, :width] + (wide[:, width:] + dot(a_rest, b_top))


def exchange(value):
    return pltpu.roll(value, value.shape[1] // 2, axis=1)


def pick(left, right):
    lane = lax.broadcasted_iota(jnp.int32, left.shape, 1)
    return jnp.where(lane < left.shape[1] // 2, left, right)


def pack(value):
    half = value.shape[0] // 2
    upper, lower = value[:half], value[half:]
    return pick(upper, exchange(lower)), pick(exchange(upper), lower)


def unpack(first, second):
    return pick(first, exchange(second)), pick(exchange(first), second)


def times_packed(matrix, y):
    half = matrix[0].shape[0] // 2
    p = times(matrix[0], matrix[1], y)
    q = times(matrix[2], matrix[3], y)
    return pick(p[:half], q[half:]) + exchange(pick(p[half:], q[:half]))


def columns(matrix):
    half = matrix.shape[1] // 2
    return split(matrix[:, :half]) + split(matrix[:, half:])


def keep(ref, matrix):
    for i, part in enumerate(columns(matrix)):
        ref[i] = part


def ring_kernel(
    sectors,
    shift_hbm, res_hbm, inv_hbm, coup_hbm, flux_hbm, lift_hbm,
    corr_ref, out_ref,
    shift_ref, res, inv, coup, flux, lift, coup4, flux4, flow4, lift4, cross4, other4, seen,
    state, landed, trace, final, above_a, above_b, beside_a, beside_b, crosses, stage, given,
    load_sem, send_sem, recv_sem, above_recv, beside_recv, trace_send,
    cross_send, cross_recv, stage_send, given_recv,
):
    row = lax.axis_index("row")
    sector = lax.axis_index("sector")
    above, beside = (above_a, above_b), (beside_a, beside_b)

    def turn(k):
        return lax.rem(sector + k, sectors)

    def remote(src, dst, send, recv, down, k):
        return pltpu.make_async_remote_copy(
            src_ref=src, dst_ref=dst, send_sem=send, recv_sem=recv,
            device_id={"row": row + down, "sector": turn(k)}, device_id_type=MESH,
        )

    pairs = [
        (flux_hbm, flux), (lift_hbm, lift), (inv_hbm, inv), (res_hbm, res), (coup_hbm, coup),
        (shift_hbm, shift_ref),
    ]
    loads = [
        pltpu.make_async_copy(src, dst, load_sem.at[i]) for i, (src, dst) in enumerate(pairs)
    ]
    for load in loads:
        load.start()

    barrier = pltpu.get_barrier_semaphore()

    def greet(up, k):
        pl.semaphore_signal(
            barrier, inc=1, device_id={"row": row - up, "sector": turn(k)}, device_id_type=MESH
        )

    greet(0, sectors - 1)

    @pl.when(row == 1)
    def _():
        for k in range(1, sectors - 1):
            greet(0, k)

    @pl.when(row % 2 == 1)
    def _():
        for k in range(sectors):
            greet(1, k)

    @pl.when(row >= 2)
    def _():
        greet(row - 1, 0)

    loads[0].wait()
    loads[1].wait()
    lift_here = lift[...].T
    cross = times(*split(flux[...]), lift_here)
    crosses[sector] = cross

    @pl.when(row % 2 == 0)
    def _():
        pl.semaphore_wait(barrier, sectors + 1)

    @pl.when(row == 1)
    def _():
        pl.semaphore_wait(barrier, sectors + 1)

    @pl.when(row == 3)
    def _():
        pl.semaphore_wait(barrier, 1)

    def cross_copies():
        return (
            lambda: [
                remote(crosses.at[sector], crosses.at[sector], cross_send.at[k], cross_recv.at[sector], 0, k)
                for k in range(1, sectors)
            ],
            lambda: [
                remote(crosses.at[sector], above_cross(sector), cross_send.at[k], cross_recv.at[sector], 1, k)
                for k in range(sectors)
            ],
        )

    def above_cross(k):
        return crosses.at[sectors + k]

    @pl.when(row == 1)
    def _():
        for copy in cross_copies()[0]():
            copy.start()

    @pl.when(row == 2)
    def _():
        for copy in cross_copies()[1]():
            copy.start()

    loads[2].wait()
    loads[3].wait()
    state[0, 0], state[0, 1] = pack(times(*split(inv[...]), res[...]))

    steps = sectors - 1

    def ring_copy(k, h):
        return remote(
            state.at[k, h], landed.at[k, h], send_sem.at[k, h], recv_sem.at[k, h], 0, 1
        )

    ring_copy(0, 0).start()
    ring_copy(0, 1).start()

    loads[4].wait()
    keep(coup4, coup[...])
    keep(flux4, flux[...])
    keep(lift4, lift_here)
    keep(cross4, cross)
    keep(flow4, times(*split(flux[...]), coup[...]))
    loads[5].wait()

    def halves(ref):
        return [ref[i] for i in range(4)]

    shift = [shift_ref[i] for i in range(3)]

    def back(by):
        return lax.rem(sector + 2 * sectors - by, sectors)

    def trace_copies(h):
        return (
            lambda: [
                remote(trace.at[h], above[h].at[sector], trace_send.at[h, k], above_recv.at[h, sector], 1, k)
                for k in range(sectors)
            ],
            lambda: [
                remote(trace.at[h], beside[h].at[sector], trace_send.at[h, k], beside_recv.at[h, sector], 0, k)
                for k in range(1, sectors)
            ],
        )

    for k in range(steps):
        for h in range(2):
            if k + 1 == steps:
                seen[h] = times_packed(halves(flux4), state[0, h])
            ring_copy(k, h).wait_recv()
            if k + 1 < steps:
                state[k + 1, h] = state[0, h] + times_packed(halves(coup4), landed[k, h])
                ring_copy(k + 1, h).start()
                continue
            trace[h] = seen[h] + times_packed(halves(flow4), landed[k, h])

            @pl.when(row % 2 == 0)
            def _():
                for copy in trace_copies(h)[0]():
                    copy.start()

            @pl.when(row == 1)
            def _():
                for copy in trace_copies(h)[1]():
                    copy.start()

            state[steps, h] = state[0, h] + times_packed(halves(coup4), landed[k, h])

        if k == 0:

            @pl.when(row == 1)
            def _():
                for i in range(1, sectors):
                    remote(
                        crosses.at[turn(i)], crosses.at[turn(i)], cross_send.at[i],
                        cross_recv.at[turn(i)], 0, i,
                    ).wait_recv()
                keep(other4.at[0], crosses[back(shift[1])])
                keep(other4.at[1], crosses[back(shift[1] + shift[2])])

            @pl.when(row == 3)
            def _():
                for i in range(sectors):
                    remote(
                        crosses.at[0], above_cross(i), cross_send.at[i], cross_recv.at[i], -1, i
                    ).wait_recv()
                keep(other4.at[0], crosses[sectors + back(shift[2])])

    def wait_above(h):
        for i in range(sectors):
            remote(
                trace.at[h], above[h].at[i], trace_send.at[h, 0], above_recv.at[h, i], -1, i
            ).wait_recv()

    def stage_copy(h, i):
        return remote(
            stage.at[h, i], given.at[h], stage_send.at[h, i], given_recv.at[h], i + 1, 0
        )

    def finish(h, moved):
        final[h] = trace[h] + times_packed(halves(cross4), moved)
        state[steps, h] += times_packed(halves(lift4), moved)

    @pl.when(row == 0)
    def _():
        final[...] = trace[...]

    @pl.when(row == 1)
    def _():
        for h in range(2):
            wait_above(h)
            for i in range(1, sectors):
                remote(
                    trace.at[h], beside[h].at[turn(i)], trace_send.at[h, i],
                    beside_recv.at[h, turn(i)], 0, i,
                ).wait_recv()
            beside[h][sector] = trace[h]
            for i, by in enumerate((shift[1], shift[1] + shift[2])):
                moved = above[h][lax.rem(back(by) + sectors - shift[0], sectors)]
                stage[h, i] = beside[h][back(by)] + times_packed(halves(other4.at[i]), moved)
                stage_copy(h, i).start()
        for h in range(2):
            finish(h, above[h][back(shift[0])])

    @pl.when(row == 2)
    def _():
        for h in range(2):
            stage_copy(h, 0).wait_recv()
            finish(h, given[h])

    @pl.when(row == 3)
    def _():
        for h in range(2):
            wait_above(h)
            stage_copy(h, 1).wait_recv()
            moved = above[h][back(shift[2])] + times_packed(halves(other4.at[0]), given[h])
            finish(h, moved)

    for ref, first, second in (
        (corr_ref, state[steps, 0], state[steps, 1]), (out_ref, final[0], final[1]),
    ):
        half = first.shape[0]
        ref[:half], ref[half:] = unpack(first, second)

    for k in range(steps):
        for h in range(2):
            ring_copy(k, h).wait_send()

    @pl.when(row % 2 == 0)
    def _():
        for h in range(2):
            for copy in trace_copies(h)[0]():
                copy.wait_send()

    @pl.when(row == 1)
    def _():
        for copy in cross_copies()[0]():
            copy.wait_send()
        for h in range(2):
            for copy in trace_copies(h)[1]():
                copy.wait_send()
            for i in range(2):
                stage_copy(h, i).wait_send()

    @pl.when(row == 2)
    def _():
        for copy in cross_copies()[1]():
            copy.wait_send()


def leave_kernel(corr_ref, out_ref, corr_hbm, out_hbm, sems):
    copies = [
        pltpu.make_async_copy(corr_ref, corr_hbm, sems.at[0]),
        pltpu.make_async_copy(out_ref, out_hbm, sems.at[1]),
    ]
    for copy in copies:
        copy.start()
    for copy in copies:
        copy.wait()


def ring_device(residual, block_inverse, cycle_coupling, outlet_flux, inlet_lift, mortar_shift):
    blk, lines = residual.shape[-2:]
    face = outlet_flux.shape[-2]
    sectors = lax.axis_size("sector")
    steps = sectors - 1
    vmem = pl.BlockSpec(memory_space=pltpu.VMEM)
    hbm = pl.BlockSpec(memory_space=pl.ANY)
    dma = pltpu.SemaphoreType.DMA
    corr, out = pl.pallas_call(
        functools.partial(ring_kernel, sectors),
        out_shape=(pltpu.VMEM((blk, lines), F32), pltpu.VMEM((face, lines), F32)),
        in_specs=[hbm] * 6,
        out_specs=(vmem, vmem),
        scratch_shapes=[
            pltpu.SMEM(mortar_shift.shape, jnp.int32),
            pltpu.VMEM((blk, lines), F32),
            pltpu.VMEM((blk, blk), F32),
            pltpu.VMEM((blk, blk), F32),
            pltpu.VMEM((face, blk), F32),
            pltpu.VMEM((face, blk), F32),
            pltpu.VMEM((4, blk, blk // 2), BF16),
            pltpu.VMEM((4, face, blk // 2), BF16),
            pltpu.VMEM((4, face, blk // 2), BF16),
            pltpu.VMEM((4, blk, face // 2), BF16),
            pltpu.VMEM((4, face, face // 2), BF16),
            pltpu.VMEM((2, 4, face, face // 2), BF16),
            pltpu.VMEM((2, face // 2, lines), F32),
            pltpu.VMEM((sectors, 2, blk // 2, lines), F32),
            pltpu.VMEM((steps, 2, blk // 2, lines), F32),
            pltpu.VMEM((2, face // 2, lines), F32),
            pltpu.VMEM((2, face // 2, lines), F32),
            pltpu.VMEM((sectors, face // 2, lines), F32),
            pltpu.VMEM((sectors, face // 2, lines), F32),
            pltpu.VMEM((sectors, face // 2, lines), F32),
            pltpu.VMEM((sectors, face // 2, lines), F32),
            pltpu.VMEM((2 * sectors, face, face), F32),
            pltpu.VMEM((2, 2, face // 2, lines), F32),
            pltpu.VMEM((2, face // 2, lines), F32),
            dma((6,)),
            dma((steps, 2)),
            dma((steps, 2)),
            dma((2, sectors)),
            dma((2, sectors)),
            dma((2, sectors)),
            dma((sectors,)),
            dma((sectors,)),
            dma((2, 2)),
            dma((2,)),
        ],
        compiler_params=pltpu.CompilerParams(
            collective_id=0, has_side_effects=True, vmem_limit_bytes=62 * 2**20
        ),
        name="ring",
    )(
        mortar_shift,
        residual.reshape(blk, lines),
        block_inverse.reshape(blk, blk),
        cycle_coupling.reshape(blk, blk),
        outlet_flux.reshape(face, blk),
        jnp.swapaxes(inlet_lift, -1, -2).reshape(face, blk),
    )
    corr, out = pl.pallas_call(
        leave_kernel,
        out_shape=(
            jax.ShapeDtypeStruct((blk, lines), F32),
            jax.ShapeDtypeStruct((face, lines), F32),
        ),
        in_specs=[hbm, hbm],
        out_specs=(hbm, hbm),
        scratch_shapes=[dma((2,))],
        compiler_params=pltpu.CompilerParams(vmem_limit_bytes=2**20),
        name="leave",
    )(corr, out)
    return corr.reshape(residual.shape), out.reshape(outlet_flux.shape[:-1] + (lines,))


def from_behind(block, axis, distance):
    devices = range(lax.axis_size(axis))
    route = [((i - distance) % len(devices), i) for i in devices]
    return lax.ppermute(block, axis, route)


def from_behind_2(value, axis, steps):
    count = lax.axis_size(axis)
    leading, last = (max(0, -steps), min(count, count - steps))
    return lax.ppermute(value, axis, [(source, source + steps) for source in range(leading, last)])


def apply_block(matrix, state):
    return jnp.einsum("ij,bjl->bil", matrix, state, precision=HIGH)


def turn_sectors(trace, offset, levels):
    for level in range(levels):
        moved = from_behind(trace, "sector", 2**level)
        trace = jnp.where(offset // 2**level % 2 == 1, moved, trace)
    return trace


def pass_down(trace):
    return from_behind_2(trace, "row", 1)


def doubling_device(residual, block_inverse, cycle_coupling, outlet_flux, inlet_lift, mortar_shift):
    res_local = residual[0, 0]
    inverse = block_inverse[0, 0]
    coupling = cycle_coupling[0, 0]
    flux = outlet_flux[0, 0]
    lift = inlet_lift[0, 0]
    source = jnp.einsum("bij,bjl->bil", inverse, res_local, precision=HIGH)
    levels = lax.axis_size("sector").bit_length() - 1
    matrix = coupling
    state = source
    for level in range(levels):
        if level + 1 < levels:
            prev_matrix, prev_state = from_behind((matrix, state), "sector", 2**level)
            state = state + apply_block(matrix, prev_state)
            matrix = jnp.dot(matrix, prev_matrix, precision=HIGH)
        else:
            prev_state = from_behind(state, "sector", 2**level)
            state = state + apply_block(matrix, prev_state)
    row_count = lax.axis_size("row")
    row_index = lax.axis_index("row")
    offset = jnp.sum(
        jnp.where(jnp.arange(row_count - 1, dtype=jnp.int32) == row_index - 1, mortar_shift, 0)
    )
    bands = state.shape[0]
    current = state
    band_ids = jnp.arange(bands, dtype=jnp.int32)
    for step in range(1, row_count + bands - 1):
        send_band = jnp.clip(step - 1 - row_index, 0, bands - 1)
        flux_one = lax.dynamic_index_in_dim(flux, send_band, 0, keepdims=False)
        state_one = lax.dynamic_index_in_dim(current, send_band, 0, keepdims=False)
        trace = jnp.dot(flux_one, state_one, precision=HIGH)[None]
        moved = turn_sectors(pass_down(trace), offset, levels)[0]
        band = step - row_index
        band_clip = jnp.clip(band, 0, bands - 1)
        lift_one = lax.dynamic_index_in_dim(lift, band_clip, 0, keepdims=False)
        solved_one = lax.dynamic_index_in_dim(state, band_clip, 0, keepdims=False)
        update = solved_one + jnp.dot(lift_one, moved, precision=HIGH)
        valid = jnp.logical_and(row_index >= 1, jnp.logical_and(band >= 0, band < bands))
        chosen = jnp.logical_and(valid, band_ids == band)[:, None, None]
        current = jnp.where(chosen, update[None], current)
    outlet = jnp.einsum("bfj,bjl->bfl", flux, current, precision=HIGH)
    return (current[None, None], outlet[None, None])


def solution(mesh):
    in_specs = (
        P("row", "sector", "band", None, None),
        P("row", "sector", "band", None, None),
        P("row", "sector", None, None),
        P("row", "sector", "band", None, None),
        P("row", "sector", "band", None, None),
        P(),
    )
    out_specs = (P("row", "sector", "band", None, None), P("row", "sector", "band", None, None))
    short = mesh.shape["sector"] <= RING_LIMIT and mesh.shape["row"] == 4
    on_device = ring_device if short else doubling_device
    return jax.shard_map(
        on_device, mesh=mesh, in_specs=in_specs, out_specs=out_specs, check_vma=False
    )
```

```python
import functools

import jax
import jax.numpy as jnp
from jax import lax
from jax.experimental import pallas as pl
from jax.experimental.pallas import tpu as pltpu
from jax.sharding import PartitionSpec as P

HIGH = lax.Precision.HIGHEST
MESH = pl.DeviceIdType.MESH
F32 = jnp.float32
BF16 = jnp.bfloat16
RING_LIMIT = 8
QUARTERS = 4


def split(value):
    top = value.astype(BF16)
    return top, (value - top.astype(F32)).astype(BF16)


def dot(a, b):
    return jnp.dot(a, b, preferred_element_type=F32)


def times(a_top, a_rest, b):
    b_top, b_rest = split(b)
    width = b.shape[1]
    wide = dot(a_top, jnp.concatenate([b_top, b_rest], axis=1))
    return wide[:, :width] + (wide[:, width:] + dot(a_rest, b_top))


def keep(ref, matrix):
    depth = matrix.shape[1]
    top, rest = split(matrix)
    ref[:, :depth] = top
    ref[:, depth : 2 * depth] = top
    ref[:, 2 * depth :] = rest


def product(kept, b):
    top, rest = split(b)
    return dot(kept[...], jnp.concatenate([top, rest, top], axis=0))


def turn_lanes(value, by):
    by %= value.shape[1]
    return pltpu.roll(value, by, axis=1) if by else value


def pack(value, parts):
    high, width = value.shape[0] // parts, value.shape[1] // parts
    lane = lax.broadcasted_iota(jnp.int32, (high, value.shape[1]), 1)
    out = value[:high]
    for i in range(1, parts):
        block = turn_lanes(value[i * high : (i + 1) * high], i * width)
        out = jnp.where(lane < i * width, out, block)
    return out


def spread(value, parts, at=0):
    width = value.shape[1] // parts
    return jnp.concatenate(
        [turn_lanes(value, (at - i) * width) for i in range(parts)], axis=0
    )


def join(left, right, width):
    lane = lax.broadcasted_iota(jnp.int32, left.shape, 1)
    return jnp.where(lane < width, left, right)


def ring_kernel(
    sectors,
    shift_hbm, res_hbm, inv_hbm, coup_hbm, flux_hbm, lift_hbm,
    corr_ref, out_ref,
    shift_ref, res, inv, coup, flux, lift, coup3, flux3, flow3, lift3, cross3, other3_a, other3_b,
    source, seen, state, landed, solved, trace, face_trace, final, above_a, above_b, beside_a, beside_b, crosses, stage, given,
    load_sem, send_sem, recv_sem, above_recv, beside_recv, trace_send,
    cross_send, cross_recv, stage_send, given_recv,
):
    row = lax.axis_index("row")
    sector = lax.axis_index("sector")
    above, beside, other3 = (above_a, above_b), (beside_a, beside_b), (other3_a, other3_b)
    lines = res.shape[1]
    quarter, half = lines // QUARTERS, lines // 2

    def turn(k):
        return lax.rem(sector + k, sectors)

    def remote(src, dst, send, recv, down, k):
        return pltpu.make_async_remote_copy(
            src_ref=src, dst_ref=dst, send_sem=send, recv_sem=recv,
            device_id={"row": row + down, "sector": turn(k)}, device_id_type=MESH,
        )

    pairs = [
        (flux_hbm, flux), (lift_hbm, lift), (inv_hbm, inv), (res_hbm, res), (coup_hbm, coup),
        (shift_hbm, shift_ref),
    ]
    loads = [
        pltpu.make_async_copy(src, dst, load_sem.at[i]) for i, (src, dst) in enumerate(pairs)
    ]
    for load in loads:
        load.start()

    barrier = pltpu.get_barrier_semaphore()

    def greet(up, k):
        pl.semaphore_signal(
            barrier, inc=1, device_id={"row": row - up, "sector": turn(k)}, device_id_type=MESH
        )

    greet(0, sectors - 1)

    @pl.when(row == 1)
    def _():
        for k in range(1, sectors - 1):
            greet(0, k)

    @pl.when(row % 2 == 1)
    def _():
        for k in range(sectors):
            greet(1, k)

    @pl.when(row >= 2)
    def _():
        greet(row - 1, 0)

    loads[0].wait()
    loads[1].wait()
    crosses[sector] = times(*split(flux[...]), lift[...].T)

    @pl.when(row % 2 == 0)
    def _():
        pl.semaphore_wait(barrier, sectors + 1)

    @pl.when(row == 1)
    def _():
        pl.semaphore_wait(barrier, sectors + 1)

    @pl.when(row == 3)
    def _():
        pl.semaphore_wait(barrier, 1)

    def cross_copies():
        return (
            lambda: [
                remote(crosses.at[sector], crosses.at[sector], cross_send.at[k], cross_recv.at[sector], 0, k)
                for k in range(1, sectors)
            ],
            lambda: [
                remote(crosses.at[sector], above_cross(sector), cross_send.at[k], cross_recv.at[sector], 1, k)
                for k in range(sectors)
            ],
        )

    def above_cross(k):
        return crosses.at[sectors + k]

    @pl.when(row == 1)
    def _():
        for copy in cross_copies()[0]():
            copy.start()

    @pl.when(row == 2)
    def _():
        for copy in cross_copies()[1]():
            copy.start()

    steps = sectors - 1

    def ring_copy(k, q):
        return remote(
            state.at[k, q], landed.at[k, q], send_sem.at[k, q], recv_sem.at[k, q], 0, 1
        )

    loads[2].wait()
    loads[3].wait()
    source[...] = times(*split(inv[...]), res[...])
    for q in range(QUARTERS):
        state[0, q] = pack(turn_lanes(source[...], -q * quarter), QUARTERS)
        ring_copy(0, q).start()

    loads[4].wait()
    keep(coup3, coup[...])
    loads[5].wait()
    shift = [shift_ref[i] for i in range(3)]

    def back(by):
        return lax.rem(sector + 2 * sectors - by, sectors)

    def ready_flux():
        keep(flux3, flux[...])
        seen[...] = product(flux3, source[...])

    def ready_flow():
        keep(flow3, times(*split(flux[...]), coup[...]))

    def ready_lift():
        keep(lift3, lift[...].T)
        keep(cross3, crosses[sector])

    def ready_other():
        @pl.when(row == 1)
        def _():
            for i in range(1, sectors):
                remote(
                    crosses.at[turn(i)], crosses.at[turn(i)], cross_send.at[i],
                    cross_recv.at[turn(i)], 0, i,
                ).wait_recv()
            keep(other3[0], crosses[back(shift[1])])
            keep(other3[1], crosses[back(shift[1] + shift[2])])

        @pl.when(row == 3)
        def _():
            for i in range(sectors):
                remote(
                    crosses.at[0], above_cross(i), cross_send.at[i], cross_recv.at[i], -1, i
                ).wait_recv()
            keep(other3[0], crosses[sectors + back(shift[2])])

    aside = [ready_flux, ready_flow, ready_lift, ready_other]

    def trace_copies(h):
        return (
            lambda: [
                remote(trace.at[h], above[h].at[sector], trace_send.at[h, k], above_recv.at[h, sector], 1, k)
                for k in range(sectors)
            ],
            lambda: [
                remote(trace.at[h], beside[h].at[sector], trace_send.at[h, k], beside_recv.at[h, sector], 0, k)
                for k in range(1, sectors)
            ],
        )

    for k in range(steps - 1):
        for q in range(QUARTERS):
            ring_copy(k, q).wait_recv()
            came = product(coup3, spread(landed[k, q], QUARTERS))
            state[k + 1, q] = state[0, q] + pack(came, QUARTERS)
            ring_copy(k + 1, q).start()
            if aside:
                aside.pop(0)()
    while aside:
        aside.pop(0)()

    def here(value, h):
        return turn_lanes(value, h * half)

    for h in range(2):
        each = range(h * QUARTERS // 2, (h + 1) * QUARTERS // 2)
        came = None
        for at, q in enumerate(each):
            ring_copy(steps - 1, q).wait_recv()
            more = spread(landed[steps - 1, q], QUARTERS, at)
            came = more if came is None else join(came, more, at * quarter)
        face_trace[h] = here(seen[...], h) + product(flow3, came)
        trace[h] = pack(face_trace[h], 2)

        @pl.when(row % 2 == 0)
        def _():
            for copy in trace_copies(h)[0]():
                copy.start()

        @pl.when(row == 1)
        def _():
            for copy in trace_copies(h)[1]():
                copy.start()

        solved[h] = here(source[...], h) + product(coup3, came)

    def wait_above(h):
        for i in range(sectors):
            remote(
                trace.at[h], above[h].at[i], trace_send.at[h, 0], above_recv.at[h, i], -1, i
            ).wait_recv()

    def stage_copy(h, i):
        return remote(
            stage.at[h, i], given.at[h], stage_send.at[h, i], given_recv.at[h], i + 1, 0
        )

    def finish(h, moved):
        moved = spread(moved, 2)
        final[h] = face_trace[h] + product(cross3, moved)
        solved[h] += product(lift3, moved)

    @pl.when(row == 0)
    def _():
        final[...] = face_trace[...]

    @pl.when(row == 1)
    def _():
        for h in range(2):
            wait_above(h)
            for i in range(1, sectors):
                remote(
                    trace.at[h], beside[h].at[turn(i)], trace_send.at[h, i],
                    beside_recv.at[h, turn(i)], 0, i,
                ).wait_recv()
            beside[h][sector] = trace[h]
            for i, by in enumerate((shift[1], shift[1] + shift[2])):
                moved = above[h][lax.rem(back(by) + sectors - shift[0], sectors)]
                stage[h, i] = beside[h][back(by)] + pack(product(other3[i], spread(moved, 2)), 2)
                stage_copy(h, i).start()
        for h in range(2):
            finish(h, above[h][back(shift[0])])

    @pl.when(row == 2)
    def _():
        for h in range(2):
            stage_copy(h, 0).wait_recv()
            finish(h, given[h])

    @pl.when(row == 3)
    def _():
        for h in range(2):
            wait_above(h)
            stage_copy(h, 1).wait_recv()
            moved = above[h][back(shift[2])] + pack(product(other3[0], spread(given[h], 2)), 2)
            finish(h, moved)

    corr_ref[...] = join(solved[0], here(solved[1], 1), half)
    out_ref[...] = join(final[0], here(final[1], 1), half)

    for k in range(steps):
        for q in range(QUARTERS):
            ring_copy(k, q).wait_send()

    @pl.when(row % 2 == 0)
    def _():
        for h in range(2):
            for copy in trace_copies(h)[0]():
                copy.wait_send()

    @pl.when(row == 1)
    def _():
        for copy in cross_copies()[0]():
            copy.wait_send()
        for h in range(2):
            for copy in trace_copies(h)[1]():
                copy.wait_send()
            for i in range(2):
                stage_copy(h, i).wait_send()

    @pl.when(row == 2)
    def _():
        for copy in cross_copies()[1]():
            copy.wait_send()


def leave_kernel(corr_ref, out_ref, corr_hbm, out_hbm, sems):
    copies = [
        pltpu.make_async_copy(corr_ref, corr_hbm, sems.at[0]),
        pltpu.make_async_copy(out_ref, out_hbm, sems.at[1]),
    ]
    for copy in copies:
        copy.start()
    for copy in copies:
        copy.wait()


def ring_device(residual, block_inverse, cycle_coupling, outlet_flux, inlet_lift, mortar_shift):
    blk, lines = residual.shape[-2:]
    face = outlet_flux.shape[-2]
    sectors = lax.axis_size("sector")
    steps = sectors - 1
    vmem = pl.BlockSpec(memory_space=pltpu.VMEM)
    hbm = pl.BlockSpec(memory_space=pl.ANY)
    dma = pltpu.SemaphoreType.DMA
    corr, out = pl.pallas_call(
        functools.partial(ring_kernel, sectors),
        out_shape=(pltpu.VMEM((blk, lines), F32), pltpu.VMEM((face, lines), F32)),
        in_specs=[hbm] * 6,
        out_specs=(vmem, vmem),
        scratch_shapes=[
            pltpu.SMEM(mortar_shift.shape, jnp.int32),
            pltpu.VMEM((blk, lines), F32),
            pltpu.VMEM((blk, blk), F32),
            pltpu.VMEM((blk, blk), F32),
            pltpu.VMEM((face, blk), F32),
            pltpu.VMEM((face, blk), F32),
            pltpu.VMEM((blk, 3 * blk), BF16),
            pltpu.VMEM((face, 3 * blk), BF16),
            pltpu.VMEM((face, 3 * blk), BF16),
            pltpu.VMEM((blk, 3 * face), BF16),
            pltpu.VMEM((face, 3 * face), BF16),
            pltpu.VMEM((face, 3 * face), BF16),
            pltpu.VMEM((face, 3 * face), BF16),
            pltpu.VMEM((blk, lines), F32),
            pltpu.VMEM((face, lines), F32),
            pltpu.VMEM((steps, QUARTERS, blk // QUARTERS, lines), F32),
            pltpu.VMEM((steps, QUARTERS, blk // QUARTERS, lines), F32),
            pltpu.VMEM((2, blk, lines), F32),
            pltpu.VMEM((2, face // 2, lines), F32),
            pltpu.VMEM((2, face, lines), F32),
            pltpu.VMEM((2, face, lines), F32),
            pltpu.VMEM((sectors, face // 2, lines), F32),
            pltpu.VMEM((sectors, face // 2, lines), F32),
            pltpu.VMEM((sectors, face // 2, lines), F32),
            pltpu.VMEM((sectors, face // 2, lines), F32),
            pltpu.VMEM((2 * sectors, face, face), F32),
            pltpu.VMEM((2, 2, face // 2, lines), F32),
            pltpu.VMEM((2, face // 2, lines), F32),
            dma((6,)),
            dma((steps, QUARTERS)),
            dma((steps, QUARTERS)),
            dma((2, sectors)),
            dma((2, sectors)),
            dma((2, sectors)),
            dma((sectors,)),
            dma((sectors,)),
            dma((2, 2)),
            dma((2,)),
        ],
        compiler_params=pltpu.CompilerParams(
            collective_id=0, has_side_effects=True, vmem_limit_bytes=62 * 2**20
        ),
        name="ring",
    )(
        mortar_shift,
        residual.reshape(blk, lines),
        block_inverse.reshape(blk, blk),
        cycle_coupling.reshape(blk, blk),
        outlet_flux.reshape(face, blk),
        jnp.swapaxes(inlet_lift, -1, -2).reshape(face, blk),
    )
    corr, out = pl.pallas_call(
        leave_kernel,
        out_shape=(
            jax.ShapeDtypeStruct((blk, lines), F32),
            jax.ShapeDtypeStruct((face, lines), F32),
        ),
        in_specs=[hbm, hbm],
        out_specs=(hbm, hbm),
        scratch_shapes=[dma((2,))],
        compiler_params=pltpu.CompilerParams(vmem_limit_bytes=2**20),
        name="leave",
    )(corr, out)
    return corr.reshape(residual.shape), out.reshape(outlet_flux.shape[:-1] + (lines,))


def from_behind(block, axis, distance):
    devices = range(lax.axis_size(axis))
    route = [((i - distance) % len(devices), i) for i in devices]
    return lax.ppermute(block, axis, route)


def from_behind_2(value, axis, steps):
    count = lax.axis_size(axis)
    leading, last = (max(0, -steps), min(count, count - steps))
    return lax.ppermute(value, axis, [(source, source + steps) for source in range(leading, last)])


def apply_block(matrix, state):
    return jnp.einsum("ij,bjl->bil", matrix, state, precision=HIGH)


def turn_sectors(trace, offset, levels):
    for level in range(levels):
        moved = from_behind(trace, "sector", 2**level)
        trace = jnp.where(offset // 2**level % 2 == 1, moved, trace)
    return trace


def pass_down(trace):
    return from_behind_2(trace, "row", 1)


def doubling_device(residual, block_inverse, cycle_coupling, outlet_flux, inlet_lift, mortar_shift):
    res_local = residual[0, 0]
    inverse = block_inverse[0, 0]
    coupling = cycle_coupling[0, 0]
    flux = outlet_flux[0, 0]
    lift = inlet_lift[0, 0]
    source = jnp.einsum("bij,bjl->bil", inverse, res_local, precision=HIGH)
    levels = lax.axis_size("sector").bit_length() - 1
    matrix = coupling
    state = source
    for level in range(levels):
        if level + 1 < levels:
            prev_matrix, prev_state = from_behind((matrix, state), "sector", 2**level)
            state = state + apply_block(matrix, prev_state)
            matrix = jnp.dot(matrix, prev_matrix, precision=HIGH)
        else:
            prev_state = from_behind(state, "sector", 2**level)
            state = state + apply_block(matrix, prev_state)
    row_count = lax.axis_size("row")
    row_index = lax.axis_index("row")
    offset = jnp.sum(
        jnp.where(jnp.arange(row_count - 1, dtype=jnp.int32) == row_index - 1, mortar_shift, 0)
    )
    bands = state.shape[0]
    current = state
    band_ids = jnp.arange(bands, dtype=jnp.int32)
    for step in range(1, row_count + bands - 1):
        send_band = jnp.clip(step - 1 - row_index, 0, bands - 1)
        flux_one = lax.dynamic_index_in_dim(flux, send_band, 0, keepdims=False)
        state_one = lax.dynamic_index_in_dim(current, send_band, 0, keepdims=False)
        trace = jnp.dot(flux_one, state_one, precision=HIGH)[None]
        moved = turn_sectors(pass_down(trace), offset, levels)[0]
        band = step - row_index
        band_clip = jnp.clip(band, 0, bands - 1)
        lift_one = lax.dynamic_index_in_dim(lift, band_clip, 0, keepdims=False)
        solved_one = lax.dynamic_index_in_dim(state, band_clip, 0, keepdims=False)
        update = solved_one + jnp.dot(lift_one, moved, precision=HIGH)
        valid = jnp.logical_and(row_index >= 1, jnp.logical_and(band >= 0, band < bands))
        chosen = jnp.logical_and(valid, band_ids == band)[:, None, None]
        current = jnp.where(chosen, update[None], current)
    outlet = jnp.einsum("bfj,bjl->bfl", flux, current, precision=HIGH)
    return (current[None, None], outlet[None, None])


def solution(mesh):
    in_specs = (
        P("row", "sector", "band", None, None),
        P("row", "sector", "band", None, None),
        P("row", "sector", None, None),
        P("row", "sector", "band", None, None),
        P("row", "sector", "band", None, None),
        P(),
    )
    out_specs = (P("row", "sector", "band", None, None), P("row", "sector", "band", None, None))
    short = mesh.shape["sector"] <= RING_LIMIT and mesh.shape["row"] == 4
    on_device = ring_device if short else doubling_device
    return jax.shard_map(
        on_device, mesh=mesh, in_specs=in_specs, out_specs=out_specs, check_vma=False
    )
```

```python
import functools

import jax
import jax.numpy as jnp
from jax import lax
from jax.experimental import pallas as pl
from jax.experimental.pallas import tpu as pltpu
from jax.sharding import PartitionSpec as P

HIGH = lax.Precision.HIGHEST
MESH = pl.DeviceIdType.MESH
F32 = jnp.float32
BF16 = jnp.bfloat16
RING_LIMIT = 8
QUARTERS = 4


def split(value):
    top = value.astype(BF16)
    return top, (value - top.astype(F32)).astype(BF16)


def dot(a, b):
    return jnp.dot(a, b, preferred_element_type=F32)


def times(a_top, a_rest, b):
    b_top, b_rest = split(b)
    width = b.shape[1]
    wide = dot(a_top, jnp.concatenate([b_top, b_rest], axis=1))
    return wide[:, :width] + (wide[:, width:] + dot(a_rest, b_top))


def keep(ref, matrix):
    depth = matrix.shape[1]
    top, rest = split(matrix)
    ref[:, :depth] = top
    ref[:, depth : 2 * depth] = top
    ref[:, 2 * depth :] = rest


def product(kept, b):
    top, rest = split(b)
    return dot(kept[...], jnp.concatenate([top, rest, top], axis=0))


def turn_lanes(value, by):
    by %= value.shape[1]
    return pltpu.roll(value, by, axis=1) if by else value


def pack(value, parts):
    high, width = value.shape[0] // parts, value.shape[1] // parts
    lane = lax.broadcasted_iota(jnp.int32, (high, value.shape[1]), 1)
    out = value[:high]
    for i in range(1, parts):
        block = turn_lanes(value[i * high : (i + 1) * high], i * width)
        out = jnp.where(lane < i * width, out, block)
    return out


def spread(value, parts, at=0):
    width = value.shape[1] // parts
    return jnp.concatenate(
        [turn_lanes(value, (at - i) * width) for i in range(parts)], axis=0
    )


def join(left, right, width):
    lane = lax.broadcasted_iota(jnp.int32, left.shape, 1)
    return jnp.where(lane < width, left, right)


def ring_kernel(
    sectors,
    shift_hbm, res_hbm, inv_hbm, coup_hbm, flux_hbm, lift_hbm,
    corr_ref, out_ref,
    shift_ref, res, inv, coup, flux, lift, coup3, flux3, flow3, lift3, cross3, other3_a, other3_b,
    source, seen, state, landed, solved, trace, face_trace, final, above_a, above_b, beside_a, beside_b, crosses, stage, given,
    load_sem, send_sem, recv_sem, above_recv, beside_recv, trace_send,
    cross_down_send, relay_send, cross_recv, stage_send, given_recv,
):
    row = lax.axis_index("row")
    sector = lax.axis_index("sector")
    above, beside, other3 = (above_a, above_b), (beside_a, beside_b), (other3_a, other3_b)
    lines = res.shape[1]
    quarter, half = lines // QUARTERS, lines // 2

    def turn(k):
        return lax.rem(sector + k, sectors)

    def remote(src, dst, send, recv, down, k):
        return pltpu.make_async_remote_copy(
            src_ref=src, dst_ref=dst, send_sem=send, recv_sem=recv,
            device_id={"row": row + down, "sector": turn(k)}, device_id_type=MESH,
        )

    pairs = [
        (inv_hbm, inv), (res_hbm, res), (coup_hbm, coup), (flux_hbm, flux), (lift_hbm, lift),
        (shift_hbm, shift_ref),
    ]
    loads = [
        pltpu.make_async_copy(src, dst, load_sem.at[i]) for i, (src, dst) in enumerate(pairs)
    ]
    for load in loads:
        load.start()

    barrier = pltpu.get_barrier_semaphore()

    def greet(up, k):
        pl.semaphore_signal(
            barrier, inc=1, device_id={"row": row - up, "sector": turn(k)}, device_id_type=MESH
        )

    greet(0, sectors - 1)

    @pl.when(row % 2 == 1)
    def _():
        for k in range(1, sectors - 1):
            greet(0, k)
        for k in range(sectors):
            greet(1, k)

    @pl.when(row >= 2)
    def _():
        greet(row - 1, 0)

    loads[0].wait()
    loads[1].wait()
    source[...] = times(*split(inv[...]), res[...])

    @pl.when(row % 2 == 0)
    def _():
        pl.semaphore_wait(barrier, sectors + 1)

    @pl.when(row == 1)
    def _():
        pl.semaphore_wait(barrier, sectors + 1)

    @pl.when(row == 3)
    def _():
        pl.semaphore_wait(barrier, sectors - 1)

    steps = sectors - 1

    def ring_copy(k, q):
        return remote(
            state.at[k, q], landed.at[k, q], send_sem.at[k, q], recv_sem.at[k, q], 0, 1
        )

    for q in range(QUARTERS):
        state[0, q] = pack(turn_lanes(source[...], -q * quarter), QUARTERS)
        ring_copy(0, q).start()

    base = row // 2 * sectors

    def cross_down():
        return remote(
            crosses.at[sector], crosses.at[sectors + sector], cross_down_send.at[0],
            cross_recv.at[sector], 1, 0,
        )

    def relay_copy(side, j):
        piece = turn(sectors - j) if side == 0 else turn(j)
        return remote(
            crosses.at[base + piece], crosses.at[base + piece], relay_send.at[side, j],
            cross_recv.at[piece], 0, 1 if side == 0 else sectors - 1,
        )

    def has_piece(side, j):
        return sector >= j if side == 0 else sector < sectors - j

    def passes_on(side, j):
        neighbour = sector < sectors - 1 if side == 0 else sector > 0
        return jnp.logical_and(row % 2 == 1, jnp.logical_and(has_piece(side, j), neighbour))

    def relay(j):
        for side in range(2):
            if j > 0:

                @pl.when(jnp.logical_and(row % 2 == 1, has_piece(side, j)))
                def _():
                    relay_copy(side, j).wait_recv()

            if j < sectors - 1:

                @pl.when(passes_on(side, j))
                def _():
                    relay_copy(side, j).start()

    loads[2].wait()
    keep(coup3, coup[...])
    loads[3].wait()
    loads[4].wait()
    crosses[sector] = times(*split(flux[...]), lift[...].T)

    @pl.when(row == 2)
    def _():
        cross_down().start()

    @pl.when(row == 3)
    def _():
        cross_down().wait_recv()

    relay(0)
    loads[5].wait()
    shift = [shift_ref[i] for i in range(3)]

    def back(by):
        return lax.rem(sector + 2 * sectors - by, sectors)

    def ready_flux():
        keep(flux3, flux[...])
        seen[...] = product(flux3, source[...])

    def ready_flow():
        keep(flow3, times(*split(flux[...]), coup[...]))

    def ready_lift():
        keep(lift3, lift[...].T)
        keep(cross3, crosses[sector])

    def ready_other():
        @pl.when(row == 1)
        def _():
            keep(other3[0], crosses[back(shift[1])])
            keep(other3[1], crosses[back(shift[1] + shift[2])])

        @pl.when(row == 3)
        def _():
            keep(other3[0], crosses[sectors + back(shift[2])])

    aside = [ready_flux, ready_flow]
    for j in range(1, sectors):
        aside.append(functools.partial(relay, j))
        if j == 1:
            aside.append(ready_lift)
    aside.append(ready_other)

    def trace_copies(h):
        return (
            lambda: [
                remote(trace.at[h], above[h].at[sector], trace_send.at[h, k], above_recv.at[h, sector], 1, k)
                for k in range(sectors)
            ],
            lambda: [
                remote(trace.at[h], beside[h].at[sector], trace_send.at[h, k], beside_recv.at[h, sector], 0, k)
                for k in range(1, sectors)
            ],
        )

    for k in range(steps - 1):
        for q in range(QUARTERS):
            ring_copy(k, q).wait_recv()
            came = product(coup3, spread(landed[k, q], QUARTERS))
            state[k + 1, q] = state[0, q] + pack(came, QUARTERS)
            ring_copy(k + 1, q).start()
            if aside:
                aside.pop(0)()
    while aside:
        aside.pop(0)()

    def here(value, h):
        return turn_lanes(value, h * half)

    for h in range(2):
        each = range(h * QUARTERS // 2, (h + 1) * QUARTERS // 2)
        came = None
        for at, q in enumerate(each):
            ring_copy(steps - 1, q).wait_recv()
            more = spread(landed[steps - 1, q], QUARTERS, at)
            came = more if came is None else join(came, more, at * quarter)
        face_trace[h] = here(seen[...], h) + product(flow3, came)
        trace[h] = pack(face_trace[h], 2)

        @pl.when(row % 2 == 0)
        def _():
            for copy in trace_copies(h)[0]():
                copy.start()

        @pl.when(row == 1)
        def _():
            for copy in trace_copies(h)[1]():
                copy.start()

        solved[h] = here(source[...], h) + product(coup3, came)

    def wait_above(h):
        for i in range(sectors):
            remote(
                trace.at[h], above[h].at[i], trace_send.at[h, 0], above_recv.at[h, i], -1, i
            ).wait_recv()

    def stage_copy(h, i):
        return remote(
            stage.at[h, i], given.at[h], stage_send.at[h, i], given_recv.at[h], i + 1, 0
        )

    def finish(h, moved):
        final[h] = face_trace[h] + product(cross3, moved)
        solved[h] += product(lift3, moved)

    @pl.when(row == 0)
    def _():
        final[...] = face_trace[...]

    @pl.when(row == 1)
    def _():
        for h in range(2):
            wait_above(h)
            for i in range(1, sectors):
                remote(
                    trace.at[h], beside[h].at[turn(i)], trace_send.at[h, i],
                    beside_recv.at[h, turn(i)], 0, i,
                ).wait_recv()
            beside[h][sector] = trace[h]
            for i, by in ((1, shift[1] + shift[2]), (0, shift[1])):
                moved = above[h][lax.rem(back(by) + sectors - shift[0], sectors)]
                stage[h, i] = beside[h][back(by)] + pack(product(other3[i], spread(moved, 2)), 2)
                stage_copy(h, i).start()
        for h in range(2):
            finish(h, spread(above[h][back(shift[0])], 2))

    @pl.when(row == 2)
    def _():
        for h in range(2):
            stage_copy(h, 0).wait_recv()
            finish(h, spread(given[h], 2))

    @pl.when(row == 3)
    def _():
        for h in range(2):
            wait_above(h)
            moved = spread(above[h][back(shift[2])], 2)
            stage_copy(h, 1).wait_recv()
            finish(h, moved + product(other3[0], spread(given[h], 2)))

    corr_ref[...] = join(solved[0], here(solved[1], 1), half)
    out_ref[...] = join(final[0], here(final[1], 1), half)

    for k in range(steps):
        for q in range(QUARTERS):
            ring_copy(k, q).wait_send()

    @pl.when(row % 2 == 0)
    def _():
        for h in range(2):
            for copy in trace_copies(h)[0]():
                copy.wait_send()

    @pl.when(row == 1)
    def _():
        for h in range(2):
            for copy in trace_copies(h)[1]():
                copy.wait_send()
            for i in range(2):
                stage_copy(h, i).wait_send()

    @pl.when(row == 2)
    def _():
        cross_down().wait_send()

    for j in range(sectors - 1):
        for side in range(2):

            @pl.when(passes_on(side, j))
            def _():
                relay_copy(side, j).wait_send()


def leave_kernel(corr_ref, out_ref, corr_hbm, out_hbm, sems):
    copies = [
        pltpu.make_async_copy(corr_ref, corr_hbm, sems.at[0]),
        pltpu.make_async_copy(out_ref, out_hbm, sems.at[1]),
    ]
    for copy in copies:
        copy.start()
    for copy in copies:
        copy.wait()


def ring_device(residual, block_inverse, cycle_coupling, outlet_flux, inlet_lift, mortar_shift):
    blk, lines = residual.shape[-2:]
    face = outlet_flux.shape[-2]
    sectors = lax.axis_size("sector")
    steps = sectors - 1
    vmem = pl.BlockSpec(memory_space=pltpu.VMEM)
    hbm = pl.BlockSpec(memory_space=pl.ANY)
    dma = pltpu.SemaphoreType.DMA
    corr, out = pl.pallas_call(
        functools.partial(ring_kernel, sectors),
        out_shape=(pltpu.VMEM((blk, lines), F32), pltpu.VMEM((face, lines), F32)),
        in_specs=[hbm] * 6,
        out_specs=(vmem, vmem),
        scratch_shapes=[
            pltpu.SMEM(mortar_shift.shape, jnp.int32),
            pltpu.VMEM((blk, lines), F32),
            pltpu.VMEM((blk, blk), F32),
            pltpu.VMEM((blk, blk), F32),
            pltpu.VMEM((face, blk), F32),
            pltpu.VMEM((face, blk), F32),
            pltpu.VMEM((blk, 3 * blk), BF16),
            pltpu.VMEM((face, 3 * blk), BF16),
            pltpu.VMEM((face, 3 * blk), BF16),
            pltpu.VMEM((blk, 3 * face), BF16),
            pltpu.VMEM((face, 3 * face), BF16),
            pltpu.VMEM((face, 3 * face), BF16),
            pltpu.VMEM((face, 3 * face), BF16),
            pltpu.VMEM((blk, lines), F32),
            pltpu.VMEM((face, lines), F32),
            pltpu.VMEM((steps, QUARTERS, blk // QUARTERS, lines), F32),
            pltpu.VMEM((steps, QUARTERS, blk // QUARTERS, lines), F32),
            pltpu.VMEM((2, blk, lines), F32),
            pltpu.VMEM((2, face // 2, lines), F32),
            pltpu.VMEM((2, face, lines), F32),
            pltpu.VMEM((2, face, lines), F32),
            pltpu.VMEM((sectors, face // 2, lines), F32),
            pltpu.VMEM((sectors, face // 2, lines), F32),
            pltpu.VMEM((sectors, face // 2, lines), F32),
            pltpu.VMEM((sectors, face // 2, lines), F32),
            pltpu.VMEM((2 * sectors, face, face), F32),
            pltpu.VMEM((2, 2, face // 2, lines), F32),
            pltpu.VMEM((2, face // 2, lines), F32),
            dma((6,)),
            dma((steps, QUARTERS)),
            dma((steps, QUARTERS)),
            dma((2, sectors)),
            dma((2, sectors)),
            dma((2, sectors)),
            dma((1,)),
            dma((2, sectors)),
            dma((sectors,)),
            dma((2, 2)),
            dma((2,)),
        ],
        compiler_params=pltpu.CompilerParams(
            collective_id=0, has_side_effects=True, vmem_limit_bytes=62 * 2**20
        ),
        name="ring",
    )(
        mortar_shift,
        residual.reshape(blk, lines),
        block_inverse.reshape(blk, blk),
        cycle_coupling.reshape(blk, blk),
        outlet_flux.reshape(face, blk),
        jnp.swapaxes(inlet_lift, -1, -2).reshape(face, blk),
    )
    corr, out = pl.pallas_call(
        leave_kernel,
        out_shape=(
            jax.ShapeDtypeStruct((blk, lines), F32),
            jax.ShapeDtypeStruct((face, lines), F32),
        ),
        in_specs=[hbm, hbm],
        out_specs=(hbm, hbm),
        scratch_shapes=[dma((2,))],
        compiler_params=pltpu.CompilerParams(vmem_limit_bytes=2**20),
        name="leave",
    )(corr, out)
    return corr.reshape(residual.shape), out.reshape(outlet_flux.shape[:-1] + (lines,))


def from_behind(block, axis, distance):
    devices = range(lax.axis_size(axis))
    route = [((i - distance) % len(devices), i) for i in devices]
    return lax.ppermute(block, axis, route)


def from_behind_2(value, axis, steps):
    count = lax.axis_size(axis)
    leading, last = (max(0, -steps), min(count, count - steps))
    return lax.ppermute(value, axis, [(source, source + steps) for source in range(leading, last)])


def apply_block(matrix, state):
    return jnp.einsum("ij,bjl->bil", matrix, state, precision=HIGH)


def turn_sectors(trace, offset, levels):
    for level in range(levels):
        moved = from_behind(trace, "sector", 2**level)
        trace = jnp.where(offset // 2**level % 2 == 1, moved, trace)
    return trace


def pass_down(trace):
    return from_behind_2(trace, "row", 1)


def doubling_device(residual, block_inverse, cycle_coupling, outlet_flux, inlet_lift, mortar_shift):
    res_local = residual[0, 0]
    inverse = block_inverse[0, 0]
    coupling = cycle_coupling[0, 0]
    flux = outlet_flux[0, 0]
    lift = inlet_lift[0, 0]
    source = jnp.einsum("bij,bjl->bil", inverse, res_local, precision=HIGH)
    levels = lax.axis_size("sector").bit_length() - 1
    matrix = coupling
    state = source
    for level in range(levels):
        if level + 1 < levels:
            prev_matrix, prev_state = from_behind((matrix, state), "sector", 2**level)
            state = state + apply_block(matrix, prev_state)
            matrix = jnp.dot(matrix, prev_matrix, precision=HIGH)
        else:
            prev_state = from_behind(state, "sector", 2**level)
            state = state + apply_block(matrix, prev_state)
    row_count = lax.axis_size("row")
    row_index = lax.axis_index("row")
    offset = jnp.sum(
        jnp.where(jnp.arange(row_count - 1, dtype=jnp.int32) == row_index - 1, mortar_shift, 0)
    )
    bands = state.shape[0]
    current = state
    band_ids = jnp.arange(bands, dtype=jnp.int32)
    for step in range(1, row_count + bands - 1):
        send_band = jnp.clip(step - 1 - row_index, 0, bands - 1)
        flux_one = lax.dynamic_index_in_dim(flux, send_band, 0, keepdims=False)
        state_one = lax.dynamic_index_in_dim(current, send_band, 0, keepdims=False)
        trace = jnp.dot(flux_one, state_one, precision=HIGH)[None]
        moved = turn_sectors(pass_down(trace), offset, levels)[0]
        band = step - row_index
        band_clip = jnp.clip(band, 0, bands - 1)
        lift_one = lax.dynamic_index_in_dim(lift, band_clip, 0, keepdims=False)
        solved_one = lax.dynamic_index_in_dim(state, band_clip, 0, keepdims=False)
        update = solved_one + jnp.dot(lift_one, moved, precision=HIGH)
        valid = jnp.logical_and(row_index >= 1, jnp.logical_and(band >= 0, band < bands))
        chosen = jnp.logical_and(valid, band_ids == band)[:, None, None]
        current = jnp.where(chosen, update[None], current)
    outlet = jnp.einsum("bfj,bjl->bfl", flux, current, precision=HIGH)
    return (current[None, None], outlet[None, None])


def solution(mesh):
    in_specs = (
        P("row", "sector", "band", None, None),
        P("row", "sector", "band", None, None),
        P("row", "sector", None, None),
        P("row", "sector", "band", None, None),
        P("row", "sector", "band", None, None),
        P(),
    )
    out_specs = (P("row", "sector", "band", None, None), P("row", "sector", "band", None, None))
    short = mesh.shape["sector"] <= RING_LIMIT and mesh.shape["row"] == 4
    on_device = ring_device if short else doubling_device
    return jax.shard_map(
        on_device, mesh=mesh, in_specs=in_specs, out_specs=out_specs, check_vma=False
    )
```

```python
import functools

import jax
import jax.numpy as jnp
from jax import lax
from jax.experimental import pallas as pl
from jax.experimental.pallas import tpu as pltpu
from jax.sharding import PartitionSpec as P

HIGH = lax.Precision.HIGHEST
MESH = pl.DeviceIdType.MESH
F32 = jnp.float32
BF16 = jnp.bfloat16
RING_LIMIT = 8
QUARTERS = 4


def split(value):
    top = value.astype(BF16)
    return top, (value - top.astype(F32)).astype(BF16)


def dot(a, b):
    return jnp.dot(a, b, preferred_element_type=F32)


def times(a_top, a_rest, b):
    b_top, b_rest = split(b)
    width = b.shape[1]
    wide = dot(a_top, jnp.concatenate([b_top, b_rest], axis=1))
    return wide[:, :width] + (wide[:, width:] + dot(a_rest, b_top))


def keep(ref, matrix):
    depth = matrix.shape[1]
    top, rest = split(matrix)
    ref[:, :depth] = top
    ref[:, depth : 2 * depth] = top
    ref[:, 2 * depth :] = rest


def product(kept, b):
    top, rest = split(b)
    return dot(kept[...], jnp.concatenate([top, rest, top], axis=0))


def turn_lanes(value, by):
    by %= value.shape[1]
    return pltpu.roll(value, by, axis=1) if by else value


def pack(value, parts):
    high, width = value.shape[0] // parts, value.shape[1] // parts
    lane = lax.broadcasted_iota(jnp.int32, (high, value.shape[1]), 1)
    out = value[:high]
    for i in range(1, parts):
        block = turn_lanes(value[i * high : (i + 1) * high], i * width)
        out = jnp.where(lane < i * width, out, block)
    return out


def spread(value, parts, at=0):
    width = value.shape[1] // parts
    return jnp.concatenate(
        [turn_lanes(value, (at - i) * width) for i in range(parts)], axis=0
    )


def join(left, right, width):
    lane = lax.broadcasted_iota(jnp.int32, left.shape, 1)
    return jnp.where(lane < width, left, right)


def ring_kernel(
    sectors,
    shift_hbm, res_hbm, inv_hbm, coup_hbm, flux_hbm, lift_hbm,
    corr_ref, out_ref,
    shift_ref, res, inv, coup, flux, lift, coup3, flux3, flow3, lift3, cross3, other3_a, other3_b,
    source, seen, state, landed, solved, trace, face_trace, final, above_a, above_b, beside_a, beside_b, crosses, stage, given,
    load_sem, send_sem, recv_sem, above_recv, beside_recv, trace_send,
    cross_send, cross_recv, stage_send, given_recv,
):
    row = lax.axis_index("row")
    sector = lax.axis_index("sector")
    above, beside, other3 = (above_a, above_b), (beside_a, beside_b), (other3_a, other3_b)
    lines = res.shape[1]
    quarter, half = lines // QUARTERS, lines // 2

    def turn(k):
        return lax.rem(sector + k, sectors)

    def remote(src, dst, send, recv, down, k):
        return pltpu.make_async_remote_copy(
            src_ref=src, dst_ref=dst, send_sem=send, recv_sem=recv,
            device_id={"row": row + down, "sector": turn(k)}, device_id_type=MESH,
        )

    pairs = [
        (inv_hbm, inv), (res_hbm, res), (coup_hbm, coup), (flux_hbm, flux), (lift_hbm, lift),
        (shift_hbm, shift_ref),
    ]
    loads = [
        pltpu.make_async_copy(src, dst, load_sem.at[i]) for i, (src, dst) in enumerate(pairs)
    ]
    for load in loads:
        load.start()

    barrier = pltpu.get_barrier_semaphore()

    def greet(up, k):
        pl.semaphore_signal(
            barrier, inc=1, device_id={"row": row - up, "sector": turn(k)}, device_id_type=MESH
        )

    greet(0, sectors - 1)

    @pl.when(row == 1)
    def _():
        for k in range(1, sectors - 1):
            greet(0, k)

    @pl.when(row % 2 == 1)
    def _():
        for k in range(sectors):
            greet(1, k)

    @pl.when(row >= 2)
    def _():
        greet(row - 1, 0)

    loads[0].wait()
    loads[1].wait()
    source[...] = times(*split(inv[...]), res[...])

    @pl.when(row % 2 == 0)
    def _():
        pl.semaphore_wait(barrier, sectors + 1)

    @pl.when(row == 1)
    def _():
        pl.semaphore_wait(barrier, sectors + 1)

    @pl.when(row == 3)
    def _():
        pl.semaphore_wait(barrier, 1)

    def cross_copies():
        return (
            lambda: [
                remote(crosses.at[sector], crosses.at[sector], cross_send.at[k], cross_recv.at[sector], 0, k)
                for k in range(1, sectors)
            ],
            lambda: [
                remote(crosses.at[sector], above_cross(sector), cross_send.at[k], cross_recv.at[sector], 1, k)
                for k in range(sectors)
            ],
        )

    def above_cross(k):
        return crosses.at[sectors + k]

    steps = sectors - 1

    def ring_copy(k, q):
        return remote(
            state.at[k, q], landed.at[k, q], send_sem.at[k, q], recv_sem.at[k, q], 0, 1
        )

    for q in range(QUARTERS):
        state[0, q] = pack(turn_lanes(source[...], -q * quarter), QUARTERS)
        ring_copy(0, q).start()

    loads[2].wait()
    keep(coup3, coup[...])
    loads[3].wait()
    loads[4].wait()
    crosses[sector] = times(*split(flux[...]), lift[...].T)

    @pl.when(row == 1)
    def _():
        for copy in cross_copies()[0]():
            copy.start()

    @pl.when(row == 2)
    def _():
        for copy in cross_copies()[1]():
            copy.start()

    loads[5].wait()
    shift = [shift_ref[i] for i in range(3)]

    def back(by):
        return lax.rem(sector + 2 * sectors - by, sectors)

    def ready_flux():
        keep(flux3, flux[...])
        seen[...] = product(flux3, source[...])

    def ready_flow():
        keep(flow3, times(*split(flux[...]), coup[...]))

    def ready_lift():
        keep(lift3, lift[...].T)
        keep(cross3, crosses[sector])

    def ready_other():
        @pl.when(row == 1)
        def _():
            for i in range(1, sectors):
                remote(
                    crosses.at[turn(i)], crosses.at[turn(i)], cross_send.at[i],
                    cross_recv.at[turn(i)], 0, i,
                ).wait_recv()
            keep(other3[0], crosses[back(shift[1])])
            keep(other3[1], crosses[back(shift[1] + shift[2])])

        @pl.when(row == 3)
        def _():
            for i in range(sectors):
                remote(
                    crosses.at[0], above_cross(i), cross_send.at[i], cross_recv.at[i], -1, i
                ).wait_recv()
            keep(other3[0], crosses[sectors + back(shift[2])])

    aside = {(0, 0): ready_flux, (0, 1): ready_flow, (0, 2): ready_lift}
    last_aside = ready_other

    def trace_copies(h):
        return (
            lambda: [
                remote(trace.at[h], above[h].at[sector], trace_send.at[h, k], above_recv.at[h, sector], 1, k)
                for k in range(sectors)
            ],
            lambda: [
                remote(trace.at[h], beside[h].at[sector], trace_send.at[h, k], beside_recv.at[h, sector], 0, k)
                for k in range(1, sectors)
            ],
        )

    for k in range(steps - 1):
        for q in range(QUARTERS):
            ring_copy(k, q).wait_recv()
            came = product(coup3, spread(landed[k, q], QUARTERS))
            state[k + 1, q] = state[0, q] + pack(came, QUARTERS)
            ring_copy(k + 1, q).start()
            if (k, q) in aside:
                aside.pop((k, q))()
    for left in aside.values():
        left()
    last_aside()

    def here(value, h):
        return turn_lanes(value, h * half)

    for h in range(2):
        each = range(h * QUARTERS // 2, (h + 1) * QUARTERS // 2)
        came = None
        for at, q in enumerate(each):
            ring_copy(steps - 1, q).wait_recv()
            more = spread(landed[steps - 1, q], QUARTERS, at)
            came = more if came is None else join(came, more, at * quarter)
        face_trace[h] = here(seen[...], h) + product(flow3, came)
        trace[h] = pack(face_trace[h], 2)

        @pl.when(row % 2 == 0)
        def _():
            for copy in trace_copies(h)[0]():
                copy.start()

        @pl.when(row == 1)
        def _():
            for copy in trace_copies(h)[1]():
                copy.start()

        solved[h] = here(source[...], h) + product(coup3, came)

    def wait_above(h):
        for i in range(sectors):
            remote(
                trace.at[h], above[h].at[i], trace_send.at[h, 0], above_recv.at[h, i], -1, i
            ).wait_recv()

    def stage_copy(h, i):
        return remote(
            stage.at[h, i], given.at[h], stage_send.at[h, i], given_recv.at[h], i + 1, 0
        )

    def finish(h, moved):
        final[h] = face_trace[h] + product(cross3, moved)
        solved[h] += product(lift3, moved)

    @pl.when(row == 0)
    def _():
        final[...] = face_trace[...]

    @pl.when(row == 1)
    def _():
        for h in range(2):
            wait_above(h)
            for i in range(1, sectors):
                remote(
                    trace.at[h], beside[h].at[turn(i)], trace_send.at[h, i],
                    beside_recv.at[h, turn(i)], 0, i,
                ).wait_recv()
            beside[h][sector] = trace[h]
            for i, by in ((1, shift[1] + shift[2]), (0, shift[1])):
                moved = above[h][lax.rem(back(by) + sectors - shift[0], sectors)]
                stage[h, i] = beside[h][back(by)] + pack(product(other3[i], spread(moved, 2)), 2)
                stage_copy(h, i).start()
        for h in range(2):
            finish(h, spread(above[h][back(shift[0])], 2))

    @pl.when(row == 2)
    def _():
        for h in range(2):
            stage_copy(h, 0).wait_recv()
            finish(h, spread(given[h], 2))

    @pl.when(row == 3)
    def _():
        for h in range(2):
            wait_above(h)
            moved = spread(above[h][back(shift[2])], 2)
            stage_copy(h, 1).wait_recv()
            finish(h, moved + product(other3[0], spread(given[h], 2)))

    corr_ref[...] = join(solved[0], here(solved[1], 1), half)
    out_ref[...] = join(final[0], here(final[1], 1), half)

    for k in range(steps):
        for q in range(QUARTERS):
            ring_copy(k, q).wait_send()

    @pl.when(row % 2 == 0)
    def _():
        for h in range(2):
            for copy in trace_copies(h)[0]():
                copy.wait_send()

    @pl.when(row == 1)
    def _():
        for copy in cross_copies()[0]():
            copy.wait_send()
        for h in range(2):
            for copy in trace_copies(h)[1]():
                copy.wait_send()
            for i in range(2):
                stage_copy(h, i).wait_send()

    @pl.when(row == 2)
    def _():
        for copy in cross_copies()[1]():
            copy.wait_send()


def leave_kernel(corr_ref, out_ref, corr_hbm, out_hbm, sems):
    copies = [
        pltpu.make_async_copy(corr_ref, corr_hbm, sems.at[0]),
        pltpu.make_async_copy(out_ref, out_hbm, sems.at[1]),
    ]
    for copy in copies:
        copy.start()
    for copy in copies:
        copy.wait()


def ring_device(residual, block_inverse, cycle_coupling, outlet_flux, inlet_lift, mortar_shift):
    blk, lines = residual.shape[-2:]
    face = outlet_flux.shape[-2]
    sectors = lax.axis_size("sector")
    steps = sectors - 1
    vmem = pl.BlockSpec(memory_space=pltpu.VMEM)
    hbm = pl.BlockSpec(memory_space=pl.ANY)
    dma = pltpu.SemaphoreType.DMA
    corr, out = pl.pallas_call(
        functools.partial(ring_kernel, sectors),
        out_shape=(pltpu.VMEM((blk, lines), F32), pltpu.VMEM((face, lines), F32)),
        in_specs=[hbm] * 6,
        out_specs=(vmem, vmem),
        scratch_shapes=[
            pltpu.SMEM(mortar_shift.shape, jnp.int32),
            pltpu.VMEM((blk, lines), F32),
            pltpu.VMEM((blk, blk), F32),
            pltpu.VMEM((blk, blk), F32),
            pltpu.VMEM((face, blk), F32),
            pltpu.VMEM((face, blk), F32),
            pltpu.VMEM((blk, 3 * blk), BF16),
            pltpu.VMEM((face, 3 * blk), BF16),
            pltpu.VMEM((face, 3 * blk), BF16),
            pltpu.VMEM((blk, 3 * face), BF16),
            pltpu.VMEM((face, 3 * face), BF16),
            pltpu.VMEM((face, 3 * face), BF16),
            pltpu.VMEM((face, 3 * face), BF16),
            pltpu.VMEM((blk, lines), F32),
            pltpu.VMEM((face, lines), F32),
            pltpu.VMEM((steps, QUARTERS, blk // QUARTERS, lines), F32),
            pltpu.VMEM((steps, QUARTERS, blk // QUARTERS, lines), F32),
            pltpu.VMEM((2, blk, lines), F32),
            pltpu.VMEM((2, face // 2, lines), F32),
            pltpu.VMEM((2, face, lines), F32),
            pltpu.VMEM((2, face, lines), F32),
            pltpu.VMEM((sectors, face // 2, lines), F32),
            pltpu.VMEM((sectors, face // 2, lines), F32),
            pltpu.VMEM((sectors, face // 2, lines), F32),
            pltpu.VMEM((sectors, face // 2, lines), F32),
            pltpu.VMEM((2 * sectors, face, face), F32),
            pltpu.VMEM((2, 2, face // 2, lines), F32),
            pltpu.VMEM((2, face // 2, lines), F32),
            dma((6,)),
            dma((steps, QUARTERS)),
            dma((steps, QUARTERS)),
            dma((2, sectors)),
            dma((2, sectors)),
            dma((2, sectors)),
            dma((sectors,)),
            dma((sectors,)),
            dma((2, 2)),
            dma((2,)),
        ],
        compiler_params=pltpu.CompilerParams(
            collective_id=0, has_side_effects=True, vmem_limit_bytes=62 * 2**20
        ),
        name="ring",
    )(
        mortar_shift,
        residual.reshape(blk, lines),
        block_inverse.reshape(blk, blk),
        cycle_coupling.reshape(blk, blk),
        outlet_flux.reshape(face, blk),
        jnp.swapaxes(inlet_lift, -1, -2).reshape(face, blk),
    )
    corr, out = pl.pallas_call(
        leave_kernel,
        out_shape=(
            jax.ShapeDtypeStruct((blk, lines), F32),
            jax.ShapeDtypeStruct((face, lines), F32),
        ),
        in_specs=[hbm, hbm],
        out_specs=(hbm, hbm),
        scratch_shapes=[dma((2,))],
        compiler_params=pltpu.CompilerParams(vmem_limit_bytes=2**20),
        name="leave",
    )(corr, out)
    return corr.reshape(residual.shape), out.reshape(outlet_flux.shape[:-1] + (lines,))


def from_behind(block, axis, distance):
    devices = range(lax.axis_size(axis))
    route = [((i - distance) % len(devices), i) for i in devices]
    return lax.ppermute(block, axis, route)


def from_behind_2(value, axis, steps):
    count = lax.axis_size(axis)
    leading, last = (max(0, -steps), min(count, count - steps))
    return lax.ppermute(value, axis, [(source, source + steps) for source in range(leading, last)])


def apply_block(matrix, state):
    return jnp.einsum("ij,bjl->bil", matrix, state, precision=HIGH)


def turn_sectors(trace, offset, levels):
    for level in range(levels):
        moved = from_behind(trace, "sector", 2**level)
        trace = jnp.where(offset // 2**level % 2 == 1, moved, trace)
    return trace


def pass_down(trace):
    return from_behind_2(trace, "row", 1)


def doubling_device(residual, block_inverse, cycle_coupling, outlet_flux, inlet_lift, mortar_shift):
    res_local = residual[0, 0]
    inverse = block_inverse[0, 0]
    coupling = cycle_coupling[0, 0]
    flux = outlet_flux[0, 0]
    lift = inlet_lift[0, 0]
    source = jnp.einsum("bij,bjl->bil", inverse, res_local, precision=HIGH)
    levels = lax.axis_size("sector").bit_length() - 1
    matrix = coupling
    state = source
    for level in range(levels):
        if level + 1 < levels:
            prev_matrix, prev_state = from_behind((matrix, state), "sector", 2**level)
            state = state + apply_block(matrix, prev_state)
            matrix = jnp.dot(matrix, prev_matrix, precision=HIGH)
        else:
            prev_state = from_behind(state, "sector", 2**level)
            state = state + apply_block(matrix, prev_state)
    row_count = lax.axis_size("row")
    row_index = lax.axis_index("row")
    offset = jnp.sum(
        jnp.where(jnp.arange(row_count - 1, dtype=jnp.int32) == row_index - 1, mortar_shift, 0)
    )
    bands = state.shape[0]
    current = state
    band_ids = jnp.arange(bands, dtype=jnp.int32)
    for step in range(1, row_count + bands - 1):
        send_band = jnp.clip(step - 1 - row_index, 0, bands - 1)
        flux_one = lax.dynamic_index_in_dim(flux, send_band, 0, keepdims=False)
        state_one = lax.dynamic_index_in_dim(current, send_band, 0, keepdims=False)
        trace = jnp.dot(flux_one, state_one, precision=HIGH)[None]
        moved = turn_sectors(pass_down(trace), offset, levels)[0]
        band = step - row_index
        band_clip = jnp.clip(band, 0, bands - 1)
        lift_one = lax.dynamic_index_in_dim(lift, band_clip, 0, keepdims=False)
        solved_one = lax.dynamic_index_in_dim(state, band_clip, 0, keepdims=False)
        update = solved_one + jnp.dot(lift_one, moved, precision=HIGH)
        valid = jnp.logical_and(row_index >= 1, jnp.logical_and(band >= 0, band < bands))
        chosen = jnp.logical_and(valid, band_ids == band)[:, None, None]
        current = jnp.where(chosen, update[None], current)
    outlet = jnp.einsum("bfj,bjl->bfl", flux, current, precision=HIGH)
    return (current[None, None], outlet[None, None])


def solution(mesh):
    in_specs = (
        P("row", "sector", "band", None, None),
        P("row", "sector", "band", None, None),
        P("row", "sector", None, None),
        P("row", "sector", "band", None, None),
        P("row", "sector", "band", None, None),
        P(),
    )
    out_specs = (P("row", "sector", "band", None, None), P("row", "sector", "band", None, None))
    short = mesh.shape["sector"] <= RING_LIMIT and mesh.shape["row"] == 4
    on_device = ring_device if short else doubling_device
    return jax.shard_map(
        on_device, mesh=mesh, in_specs=in_specs, out_specs=out_specs, check_vma=False
    )
```

```python
import functools

import jax
import jax.numpy as jnp
from jax import lax
from jax.experimental import pallas as pl
from jax.experimental.pallas import tpu as pltpu
from jax.sharding import PartitionSpec as P

HIGH = lax.Precision.HIGHEST
MESH = pl.DeviceIdType.MESH
F32 = jnp.float32
BF16 = jnp.bfloat16
RING_LIMIT = 8
QUARTERS = 4


def split(value):
    top = value.astype(BF16)
    return top, (value - top.astype(F32)).astype(BF16)


def dot(a, b):
    return jnp.dot(a, b, preferred_element_type=F32)


def times(a_top, a_rest, b):
    b_top, b_rest = split(b)
    width = b.shape[1]
    wide = dot(a_top, jnp.concatenate([b_top, b_rest], axis=1))
    return wide[:, :width] + (wide[:, width:] + dot(a_rest, b_top))


def keep(ref, matrix):
    depth = matrix.shape[1]
    top, rest = split(matrix)
    ref[:, :depth] = top
    ref[:, depth : 2 * depth] = top
    ref[:, 2 * depth :] = rest


def product(kept, b):
    top, rest = split(b)
    return dot(kept[...], jnp.concatenate([top, rest, top], axis=0))


def turn_lanes(value, by):
    by %= value.shape[1]
    return pltpu.roll(value, by, axis=1) if by else value


def pack(value, parts):
    high, width = value.shape[0] // parts, value.shape[1] // parts
    lane = lax.broadcasted_iota(jnp.int32, (high, value.shape[1]), 1)
    out = value[:high]
    for i in range(1, parts):
        block = turn_lanes(value[i * high : (i + 1) * high], i * width)
        out = jnp.where(lane < i * width, out, block)
    return out


def spread(value, parts, at=0):
    width = value.shape[1] // parts
    return jnp.concatenate(
        [turn_lanes(value, (at - i) * width) for i in range(parts)], axis=0
    )


def join(left, right, width):
    lane = lax.broadcasted_iota(jnp.int32, left.shape, 1)
    return jnp.where(lane < width, left, right)


def ring_kernel(
    sectors,
    shift_hbm, res_hbm, inv_hbm, coup_hbm, flux_hbm, lift_hbm,
    corr_ref, out_ref,
    shift_ref, res, inv, coup, flux, lift, coup3, flux3, flow3, end3, other3_a, other3_b,
    source, seen, state, landed, solved, trace, face_trace, final, above_a, above_b, beside_a, beside_b, crosses, stage, given,
    load_sem, send_sem, recv_sem, above_recv, beside_recv, trace_send,
    cross_send, cross_recv, stage_send, given_recv,
):
    row = lax.axis_index("row")
    sector = lax.axis_index("sector")
    above, beside, other3 = (above_a, above_b), (beside_a, beside_b), (other3_a, other3_b)
    lines = res.shape[1]
    quarter, half = lines // QUARTERS, lines // 2
    depth, face = coup.shape[1], flux.shape[0]

    def turn(k):
        return lax.rem(sector + k, sectors)

    def remote(src, dst, send, recv, down, k):
        return pltpu.make_async_remote_copy(
            src_ref=src, dst_ref=dst, send_sem=send, recv_sem=recv,
            device_id={"row": row + down, "sector": turn(k)}, device_id_type=MESH,
        )

    pairs = [
        (inv_hbm, inv), (res_hbm, res), (coup_hbm, coup), (flux_hbm, flux), (lift_hbm, lift),
        (shift_hbm, shift_ref),
    ]
    loads = [
        pltpu.make_async_copy(src, dst, load_sem.at[i]) for i, (src, dst) in enumerate(pairs)
    ]
    for load in loads:
        load.start()

    barrier = pltpu.get_barrier_semaphore()

    def greet(up, k):
        pl.semaphore_signal(
            barrier, inc=1, device_id={"row": row - up, "sector": turn(k)}, device_id_type=MESH
        )

    greet(0, sectors - 1)

    @pl.when(row == 1)
    def _():
        for k in range(1, sectors - 1):
            greet(0, k)

    @pl.when(row % 2 == 1)
    def _():
        for k in range(sectors):
            greet(1, k)

    @pl.when(row >= 2)
    def _():
        greet(row - 1, 0)

    loads[0].wait()
    loads[1].wait()
    source[...] = times(*split(inv[...]), res[...])

    @pl.when(row % 2 == 0)
    def _():
        pl.semaphore_wait(barrier, sectors + 1)

    @pl.when(row == 1)
    def _():
        pl.semaphore_wait(barrier, sectors + 1)

    @pl.when(row == 3)
    def _():
        pl.semaphore_wait(barrier, 1)

    def cross_copies():
        return (
            lambda: [
                remote(crosses.at[sector], crosses.at[sector], cross_send.at[k], cross_recv.at[sector], 0, k)
                for k in range(1, sectors)
            ],
            lambda: [
                remote(crosses.at[sector], above_cross(sector), cross_send.at[k], cross_recv.at[sector], 1, k)
                for k in range(sectors)
            ],
        )

    def above_cross(k):
        return crosses.at[sectors + k]

    steps = sectors - 1

    def ring_copy(k, q):
        return remote(
            state.at[k, q], landed.at[k, q], send_sem.at[k, q], recv_sem.at[k, q], 0, 1
        )

    for q in range(QUARTERS):
        state[0, q] = pack(turn_lanes(source[...], -q * quarter), QUARTERS)
        ring_copy(0, q).start()

    loads[2].wait()
    keep(coup3, coup[...])
    loads[3].wait()
    loads[4].wait()
    crosses[sector] = times(*split(flux[...]), lift[...].T)

    @pl.when(row == 1)
    def _():
        for copy in cross_copies()[0]():
            copy.start()

    @pl.when(row == 2)
    def _():
        for copy in cross_copies()[1]():
            copy.start()

    loads[5].wait()
    shift = [shift_ref[i] for i in range(3)]

    def back(by):
        return lax.rem(sector + 2 * sectors - by, sectors)

    def ready_flux():
        keep(flux3, flux[...])
        seen[...] = product(flux3, source[...])

    def ready_flow():
        flux_top, flux_rest = split(flux[...])
        coup_top, coup_rest = coup3[:, :depth], coup3[:, 2 * depth :]
        rest = dot(flux_top, coup_rest) + dot(flux_rest, coup_top)
        keep(flow3, dot(flux_top, coup_top) + rest)

    def ready_lift():
        keep(end3, jnp.concatenate([lift[...].T, crosses[sector]], axis=0))

    def ready_other():
        @pl.when(row == 1)
        def _():
            for i in range(1, sectors):
                remote(
                    crosses.at[turn(i)], crosses.at[turn(i)], cross_send.at[i],
                    cross_recv.at[turn(i)], 0, i,
                ).wait_recv()
            keep(other3[0], crosses[back(shift[1])])
            keep(other3[1], crosses[back(shift[1] + shift[2])])

        @pl.when(row == 3)
        def _():
            for i in range(sectors):
                remote(
                    crosses.at[0], above_cross(i), cross_send.at[i], cross_recv.at[i], -1, i
                ).wait_recv()
            keep(other3[0], crosses[sectors + back(shift[2])])

    ready_flux()
    last = QUARTERS - 1
    aside = {(0, last - 1): ready_flow, (0, last): ready_lift, (1, last): ready_other}

    far_first = sorted(range(1, sectors), key=lambda k: abs(2 * k - sectors)) + [0]

    def trace_copies(h):
        return (
            lambda: [
                remote(trace.at[h], above[h].at[sector], trace_send.at[h, k], above_recv.at[h, sector], 1, k)
                for k in far_first
            ],
            lambda: [
                remote(trace.at[h], beside[h].at[sector], trace_send.at[h, k], beside_recv.at[h, sector], 0, k)
                for k in far_first[:-1]
            ],
        )

    for k in range(steps - 1):
        for q in range(QUARTERS):
            ring_copy(k, q).wait_recv()
            came = product(coup3, spread(landed[k, q], QUARTERS))
            state[k + 1, q] = state[0, q] + pack(came, QUARTERS)
            ring_copy(k + 1, q).start()
            if (k, q) in aside:
                aside.pop((k, q))()
    for left in aside.values():
        left()

    def here(value, h):
        return turn_lanes(value, h * half)

    for h in range(2):
        each = range(h * QUARTERS // 2, (h + 1) * QUARTERS // 2)
        came = None
        for at, q in enumerate(each):
            ring_copy(steps - 1, q).wait_recv()
            more = spread(landed[steps - 1, q], QUARTERS, at)
            came = more if came is None else join(came, more, at * quarter)
        face_trace[h] = here(seen[...], h) + product(flow3, came)
        trace[h] = pack(face_trace[h], 2)

        @pl.when(row % 2 == 0)
        def _():
            for copy in trace_copies(h)[0]():
                copy.start()

        @pl.when(row == 1)
        def _():
            for copy in trace_copies(h)[1]():
                copy.start()

        solved[h] = here(source[...], h) + product(coup3, came)

    def wait_above(h):
        for i in range(sectors):
            remote(
                trace.at[h], above[h].at[i], trace_send.at[h, 0], above_recv.at[h, i], -1, i
            ).wait_recv()

    def stage_copy(h, i):
        return remote(
            stage.at[h, i], given.at[h], stage_send.at[h, i], given_recv.at[h], i + 1, 0
        )

    def finish(h, moved):
        both = product(end3, moved)
        solved[h] += both[:depth]
        final[h] = face_trace[h] + both[depth:]

    @pl.when(row == 0)
    def _():
        final[...] = face_trace[...]

    @pl.when(row == 1)
    def _():
        for h in range(2):
            wait_above(h)
            for i in range(1, sectors):
                remote(
                    trace.at[h], beside[h].at[turn(i)], trace_send.at[h, i],
                    beside_recv.at[h, turn(i)], 0, i,
                ).wait_recv()
            beside[h][sector] = trace[h]
            for i, by in ((1, shift[1] + shift[2]), (0, shift[1])):
                moved = above[h][lax.rem(back(by) + sectors - shift[0], sectors)]
                stage[h, i] = beside[h][back(by)] + pack(product(other3[i], spread(moved, 2)), 2)
                stage_copy(h, i).start()
        for h in range(2):
            finish(h, spread(above[h][back(shift[0])], 2))

    @pl.when(row == 2)
    def _():
        for h in range(2):
            stage_copy(h, 0).wait_recv()
            finish(h, spread(given[h], 2))

    @pl.when(row == 3)
    def _():
        for h in range(2):
            wait_above(h)
            moved = spread(above[h][back(shift[2])], 2)
            stage_copy(h, 1).wait_recv()
            finish(h, moved + product(other3[0], spread(given[h], 2)))

    corr_ref[...] = join(solved[0], here(solved[1], 1), half)
    out_ref[...] = join(final[0], here(final[1], 1), half)

    for k in range(steps):
        for q in range(QUARTERS):
            ring_copy(k, q).wait_send()

    @pl.when(row % 2 == 0)
    def _():
        for h in range(2):
            for copy in trace_copies(h)[0]():
                copy.wait_send()

    @pl.when(row == 1)
    def _():
        for copy in cross_copies()[0]():
            copy.wait_send()
        for h in range(2):
            for copy in trace_copies(h)[1]():
                copy.wait_send()
            for i in range(2):
                stage_copy(h, i).wait_send()

    @pl.when(row == 2)
    def _():
        for copy in cross_copies()[1]():
            copy.wait_send()


def leave_kernel(corr_ref, out_ref, corr_hbm, out_hbm, sems):
    copies = [
        pltpu.make_async_copy(corr_ref, corr_hbm, sems.at[0]),
        pltpu.make_async_copy(out_ref, out_hbm, sems.at[1]),
    ]
    for copy in copies:
        copy.start()
    for copy in copies:
        copy.wait()


def ring_device(residual, block_inverse, cycle_coupling, outlet_flux, inlet_lift, mortar_shift):
    blk, lines = residual.shape[-2:]
    face = outlet_flux.shape[-2]
    sectors = lax.axis_size("sector")
    steps = sectors - 1
    vmem = pl.BlockSpec(memory_space=pltpu.VMEM)
    hbm = pl.BlockSpec(memory_space=pl.ANY)
    dma = pltpu.SemaphoreType.DMA
    corr, out = pl.pallas_call(
        functools.partial(ring_kernel, sectors),
        out_shape=(pltpu.VMEM((blk, lines), F32), pltpu.VMEM((face, lines), F32)),
        in_specs=[hbm] * 6,
        out_specs=(vmem, vmem),
        scratch_shapes=[
            pltpu.SMEM(mortar_shift.shape, jnp.int32),
            pltpu.VMEM((blk, lines), F32),
            pltpu.VMEM((blk, blk), F32),
            pltpu.VMEM((blk, blk), F32),
            pltpu.VMEM((face, blk), F32),
            pltpu.VMEM((face, blk), F32),
            pltpu.VMEM((blk, 3 * blk), BF16),
            pltpu.VMEM((face, 3 * blk), BF16),
            pltpu.VMEM((face, 3 * blk), BF16),
            pltpu.VMEM((blk + face, 3 * face), BF16),
            pltpu.VMEM((face, 3 * face), BF16),
            pltpu.VMEM((face, 3 * face), BF16),
            pltpu.VMEM((blk, lines), F32),
            pltpu.VMEM((face, lines), F32),
            pltpu.VMEM((steps, QUARTERS, blk // QUARTERS, lines), F32),
            pltpu.VMEM((steps, QUARTERS, blk // QUARTERS, lines), F32),
            pltpu.VMEM((2, blk, lines), F32),
            pltpu.VMEM((2, face // 2, lines), F32),
            pltpu.VMEM((2, face, lines), F32),
            pltpu.VMEM((2, face, lines), F32),
            pltpu.VMEM((sectors, face // 2, lines), F32),
            pltpu.VMEM((sectors, face // 2, lines), F32),
            pltpu.VMEM((sectors, face // 2, lines), F32),
            pltpu.VMEM((sectors, face // 2, lines), F32),
            pltpu.VMEM((2 * sectors, face, face), F32),
            pltpu.VMEM((2, 2, face // 2, lines), F32),
            pltpu.VMEM((2, face // 2, lines), F32),
            dma((6,)),
            dma((steps, QUARTERS)),
            dma((steps, QUARTERS)),
            dma((2, sectors)),
            dma((2, sectors)),
            dma((2, sectors)),
            dma((sectors,)),
            dma((sectors,)),
            dma((2, 2)),
            dma((2,)),
        ],
        compiler_params=pltpu.CompilerParams(
            collective_id=0, has_side_effects=True, vmem_limit_bytes=62 * 2**20
        ),
        name="ring",
    )(
        mortar_shift,
        residual.reshape(blk, lines),
        block_inverse.reshape(blk, blk),
        cycle_coupling.reshape(blk, blk),
        outlet_flux.reshape(face, blk),
        jnp.swapaxes(inlet_lift, -1, -2).reshape(face, blk),
    )
    corr, out = pl.pallas_call(
        leave_kernel,
        out_shape=(
            jax.ShapeDtypeStruct((blk, lines), F32),
            jax.ShapeDtypeStruct((face, lines), F32),
        ),
        in_specs=[hbm, hbm],
        out_specs=(hbm, hbm),
        scratch_shapes=[dma((2,))],
        compiler_params=pltpu.CompilerParams(vmem_limit_bytes=2**20),
        name="leave",
    )(corr, out)
    return corr.reshape(residual.shape), out.reshape(outlet_flux.shape[:-1] + (lines,))


def from_behind(block, axis, distance):
    devices = range(lax.axis_size(axis))
    route = [((i - distance) % len(devices), i) for i in devices]
    return lax.ppermute(block, axis, route)


def from_behind_2(value, axis, steps):
    count = lax.axis_size(axis)
    leading, last = (max(0, -steps), min(count, count - steps))
    return lax.ppermute(value, axis, [(source, source + steps) for source in range(leading, last)])


def apply_block(matrix, state):
    return jnp.einsum("ij,bjl->bil", matrix, state, precision=HIGH)


def turn_sectors(trace, offset, levels):
    for level in range(levels):
        moved = from_behind(trace, "sector", 2**level)
        trace = jnp.where(offset // 2**level % 2 == 1, moved, trace)
    return trace


def pass_down(trace):
    return from_behind_2(trace, "row", 1)


def doubling_device(residual, block_inverse, cycle_coupling, outlet_flux, inlet_lift, mortar_shift):
    res_local = residual[0, 0]
    inverse = block_inverse[0, 0]
    coupling = cycle_coupling[0, 0]
    flux = outlet_flux[0, 0]
    lift = inlet_lift[0, 0]
    source = jnp.einsum("bij,bjl->bil", inverse, res_local, precision=HIGH)
    levels = lax.axis_size("sector").bit_length() - 1
    matrix = coupling
    state = source
    for level in range(levels):
        if level + 1 < levels:
            prev_matrix, prev_state = from_behind((matrix, state), "sector", 2**level)
            state = state + apply_block(matrix, prev_state)
            matrix = jnp.dot(matrix, prev_matrix, precision=HIGH)
        else:
            prev_state = from_behind(state, "sector", 2**level)
            state = state + apply_block(matrix, prev_state)
    row_count = lax.axis_size("row")
    row_index = lax.axis_index("row")
    offset = jnp.sum(
        jnp.where(jnp.arange(row_count - 1, dtype=jnp.int32) == row_index - 1, mortar_shift, 0)
    )
    bands = state.shape[0]
    current = state
    band_ids = jnp.arange(bands, dtype=jnp.int32)
    for step in range(1, row_count + bands - 1):
        send_band = jnp.clip(step - 1 - row_index, 0, bands - 1)
        flux_one = lax.dynamic_index_in_dim(flux, send_band, 0, keepdims=False)
        state_one = lax.dynamic_index_in_dim(current, send_band, 0, keepdims=False)
        trace = jnp.dot(flux_one, state_one, precision=HIGH)[None]
        moved = turn_sectors(pass_down(trace), offset, levels)[0]
        band = step - row_index
        band_clip = jnp.clip(band, 0, bands - 1)
        lift_one = lax.dynamic_index_in_dim(lift, band_clip, 0, keepdims=False)
        solved_one = lax.dynamic_index_in_dim(state, band_clip, 0, keepdims=False)
        update = solved_one + jnp.dot(lift_one, moved, precision=HIGH)
        valid = jnp.logical_and(row_index >= 1, jnp.logical_and(band >= 0, band < bands))
        chosen = jnp.logical_and(valid, band_ids == band)[:, None, None]
        current = jnp.where(chosen, update[None], current)
    outlet = jnp.einsum("bfj,bjl->bfl", flux, current, precision=HIGH)
    return (current[None, None], outlet[None, None])


def solution(mesh):
    in_specs = (
        P("row", "sector", "band", None, None),
        P("row", "sector", "band", None, None),
        P("row", "sector", None, None),
        P("row", "sector", "band", None, None),
        P("row", "sector", "band", None, None),
        P(),
    )
    out_specs = (P("row", "sector", "band", None, None), P("row", "sector", "band", None, None))
    short = mesh.shape["sector"] <= RING_LIMIT and mesh.shape["row"] == 4
    on_device = ring_device if short else doubling_device
    return jax.shard_map(
        on_device, mesh=mesh, in_specs=in_specs, out_specs=out_specs, check_vma=False
    )
```

```python
import functools

import jax
import jax.numpy as jnp
from jax import lax
from jax.experimental import pallas as pl
from jax.experimental.pallas import tpu as pltpu
from jax.sharding import PartitionSpec as P

HIGH = lax.Precision.HIGHEST
MESH = pl.DeviceIdType.MESH
F32 = jnp.float32
BF16 = jnp.bfloat16
RING_LIMIT = 8
QUARTERS = 4


def split(value):
    top = value.astype(BF16)
    return top, (value - top.astype(F32)).astype(BF16)


def dot(a, b):
    return jnp.dot(a, b, preferred_element_type=F32)


def times(a_top, a_rest, b):
    b_top, b_rest = split(b)
    width = b.shape[1]
    wide = dot(a_top, jnp.concatenate([b_top, b_rest], axis=1))
    return wide[:, :width] + (wide[:, width:] + dot(a_rest, b_top))


def keep(ref, matrix):
    depth = matrix.shape[1]
    top, rest = split(matrix)
    ref[:, :depth] = top
    ref[:, depth : 2 * depth] = top
    ref[:, 2 * depth :] = rest


def product(kept, b):
    top, rest = split(b)
    return dot(kept[...], jnp.concatenate([top, rest, top], axis=0))


def turn_lanes(value, by):
    by %= value.shape[1]
    return pltpu.roll(value, by, axis=1) if by else value


def pack(value, parts):
    high, width = value.shape[0] // parts, value.shape[1] // parts
    lane = lax.broadcasted_iota(jnp.int32, (high, value.shape[1]), 1)
    out = value[:high]
    for i in range(1, parts):
        block = turn_lanes(value[i * high : (i + 1) * high], i * width)
        out = jnp.where(lane < i * width, out, block)
    return out


def spread(value, parts, at=0):
    width = value.shape[1] // parts
    return jnp.concatenate(
        [turn_lanes(value, (at - i) * width) for i in range(parts)], axis=0
    )


def join(left, right, width):
    lane = lax.broadcasted_iota(jnp.int32, left.shape, 1)
    return jnp.where(lane < width, left, right)


def ring_kernel(
    sectors,
    shift_hbm, res_hbm, inv_hbm, coup_hbm, flux_hbm, lift_hbm,
    corr_ref, out_ref,
    shift_ref, res, inv, coup, flux, lift, coup3, flux3, flow3, end3, other3_a, other3_b,
    source, seen, state, landed, solved, trace, face_trace, final, above_a, above_b, beside_a, beside_b, crosses, stage, given,
    load_sem, send_sem, recv_sem, above_recv, beside_recv, trace_send,
    cross_down_send, relay_send, cross_recv, stage_send, given_recv,
):
    row = lax.axis_index("row")
    sector = lax.axis_index("sector")
    above, beside, other3 = (above_a, above_b), (beside_a, beside_b), (other3_a, other3_b)
    lines = res.shape[1]
    quarter, half = lines // QUARTERS, lines // 2
    depth, face = coup.shape[1], flux.shape[0]

    def turn(k):
        return lax.rem(sector + k, sectors)

    def remote(src, dst, send, recv, down, k):
        return pltpu.make_async_remote_copy(
            src_ref=src, dst_ref=dst, send_sem=send, recv_sem=recv,
            device_id={"row": row + down, "sector": turn(k)}, device_id_type=MESH,
        )

    high = inv.shape[0] // QUARTERS
    blocks = [pl.ds(i * high, high) for i in range(QUARTERS)]
    pairs = [
        (res_hbm, res), (coup_hbm, coup), (flux_hbm, flux), (lift_hbm, lift),
        (shift_hbm, shift_ref),
    ]
    pairs[1:1] = [(inv_hbm.at[block], inv.at[block]) for block in blocks]
    loads = [
        pltpu.make_async_copy(src, dst, load_sem.at[i]) for i, (src, dst) in enumerate(pairs)
    ]
    for load in loads:
        load.start()

    barrier = pltpu.get_barrier_semaphore()

    def greet(up, k):
        pl.semaphore_signal(
            barrier, inc=1, device_id={"row": row - up, "sector": turn(k)}, device_id_type=MESH
        )

    greet(0, sectors - 1)

    @pl.when(row % 2 == 1)
    def _():
        for k in range(1, sectors - 1):
            greet(0, k)

    @pl.when(row % 2 == 1)
    def _():
        for k in range(sectors):
            greet(1, k)

    @pl.when(row >= 2)
    def _():
        greet(row - 1, 0)

    loads.pop(0).wait()
    for block in blocks:
        loads.pop(0).wait()
        source[block] = times(*split(inv[block]), res[...])

    @pl.when(row % 2 == 0)
    def _():
        pl.semaphore_wait(barrier, sectors + 1)

    @pl.when(row == 1)
    def _():
        pl.semaphore_wait(barrier, sectors + 1)

    @pl.when(row == 3)
    def _():
        pl.semaphore_wait(barrier, sectors - 1)

    steps = sectors - 1

    def ring_copy(k, q):
        return remote(
            state.at[k, q], landed.at[k, q], send_sem.at[k, q], recv_sem.at[k, q], 0, 1
        )

    for q in range(QUARTERS):
        state[0, q] = pack(turn_lanes(source[...], -q * quarter), QUARTERS)
        ring_copy(0, q).start()

    base = row // 2 * sectors

    def cross_down():
        return remote(
            crosses.at[sector], crosses.at[sectors + sector], cross_down_send.at[0],
            cross_recv.at[sector], 1, 0,
        )

    def relay_copy(side, j):
        piece = turn(sectors - j) if side == 0 else turn(j)
        return remote(
            crosses.at[base + piece], crosses.at[base + piece], relay_send.at[side, j],
            cross_recv.at[piece], 0, 1 if side == 0 else sectors - 1,
        )

    def has_piece(side, j):
        return sector >= j if side == 0 else sector < sectors - j

    def passes_on(side, j):
        neighbour = sector < sectors - 1 if side == 0 else sector > 0
        return jnp.logical_and(row % 2 == 1, jnp.logical_and(has_piece(side, j), neighbour))

    def relay(j):
        for side in range(2):
            if j > 0:

                @pl.when(jnp.logical_and(row % 2 == 1, has_piece(side, j)))
                def _():
                    relay_copy(side, j).wait_recv()

            if j < sectors - 1:

                @pl.when(passes_on(side, j))
                def _():
                    relay_copy(side, j).start()

    loads[0].wait()
    keep(coup3, coup[...])
    loads[1].wait()
    loads[2].wait()
    crosses[sector] = times(*split(flux[...]), lift[...].T)

    @pl.when(row == 2)
    def _():
        cross_down().start()

    @pl.when(row == 1)
    def _():
        relay(0)

    loads[3].wait()
    shift = [shift_ref[i] for i in range(3)]

    def back(by):
        return lax.rem(sector + 2 * sectors - by, sectors)

    def ready_flux():
        keep(flux3, flux[...])
        seen[...] = product(flux3, source[...])

    def ready_flow():
        flux_top, flux_rest = split(flux[...])
        coup_top, coup_rest = coup3[:, :depth], coup3[:, 2 * depth :]
        rest = dot(flux_top, coup_rest) + dot(flux_rest, coup_top)
        keep(flow3, dot(flux_top, coup_top) + rest)

    def ready_lift():
        keep(end3, jnp.concatenate([lift[...].T, crosses[sector]], axis=0))

    def relay_first():
        @pl.when(row == 3)
        def _():
            cross_down().wait_recv()
            relay(0)

    def ready_other():
        @pl.when(row == 1)
        def _():
            keep(other3[0], crosses[back(shift[1])])
            keep(other3[1], crosses[back(shift[1] + shift[2])])

        @pl.when(row == 3)
        def _():
            keep(other3[0], crosses[sectors + back(shift[2])])

    ready_flux()
    aside = [
        None, relay_first, ready_flow, ready_lift, functools.partial(relay, 1), None, None,
        functools.partial(relay, 2),
    ]

    far_first = sorted(range(1, sectors), key=lambda k: abs(2 * k - sectors)) + [0]

    def trace_copies(h):
        return (
            lambda: [
                remote(trace.at[h], above[h].at[sector], trace_send.at[h, k], above_recv.at[h, sector], 1, k)
                for k in far_first
            ],
            lambda: [
                remote(trace.at[h], beside[h].at[sector], trace_send.at[h, k], beside_recv.at[h, sector], 0, k)
                for k in far_first[:-1]
            ],
        )

    for k in range(steps - 1):
        for q in range(QUARTERS):
            ring_copy(k, q).wait_recv()
            came = product(coup3, spread(landed[k, q], QUARTERS))
            state[k + 1, q] = state[0, q] + pack(came, QUARTERS)
            ring_copy(k + 1, q).start()
            if aside:
                (aside.pop(0) or (lambda: None))()
    for left in aside:
        if left:
            left()

    def here(value, h):
        return turn_lanes(value, h * half)

    for h in range(2):
        each = range(h * QUARTERS // 2, (h + 1) * QUARTERS // 2)
        came = None
        for at, q in enumerate(each):
            ring_copy(steps - 1, q).wait_recv()
            more = spread(landed[steps - 1, q], QUARTERS, at)
            came = more if came is None else join(came, more, at * quarter)
        face_trace[h] = here(seen[...], h) + product(flow3, came)
        trace[h] = pack(face_trace[h], 2)

        @pl.when(row % 2 == 0)
        def _():
            for copy in trace_copies(h)[0]():
                copy.start()

        @pl.when(row == 1)
        def _():
            for copy in trace_copies(h)[1]():
                copy.start()

        solved[h] = here(source[...], h) + product(coup3, came)
        if h == 0:
            for j in range(min(3, sectors), sectors):
                relay(j)
            ready_other()

    def wait_above(h):
        for i in range(sectors):
            remote(
                trace.at[h], above[h].at[i], trace_send.at[h, 0], above_recv.at[h, i], -1, i
            ).wait_recv()

    def stage_copy(h, i):
        return remote(
            stage.at[h, i], given.at[h], stage_send.at[h, i], given_recv.at[h], i + 1, 0
        )

    def finish(h, moved):
        both = product(end3, moved)
        solved[h] += both[:depth]
        final[h] = face_trace[h] + both[depth:]

    @pl.when(row == 0)
    def _():
        final[...] = face_trace[...]

    @pl.when(row == 1)
    def _():
        for h in range(2):
            wait_above(h)
            for i in range(1, sectors):
                remote(
                    trace.at[h], beside[h].at[turn(i)], trace_send.at[h, i],
                    beside_recv.at[h, turn(i)], 0, i,
                ).wait_recv()
            beside[h][sector] = trace[h]
            for i, by in ((1, shift[1] + shift[2]), (0, shift[1])):
                moved = above[h][lax.rem(back(by) + sectors - shift[0], sectors)]
                stage[h, i] = beside[h][back(by)] + pack(product(other3[i], spread(moved, 2)), 2)
                stage_copy(h, i).start()
        for h in range(2):
            finish(h, spread(above[h][back(shift[0])], 2))

    @pl.when(row == 2)
    def _():
        for h in range(2):
            stage_copy(h, 0).wait_recv()
            finish(h, spread(given[h], 2))

    @pl.when(row == 3)
    def _():
        for h in range(2):
            wait_above(h)
            moved = spread(above[h][back(shift[2])], 2)
            stage_copy(h, 1).wait_recv()
            finish(h, moved + product(other3[0], spread(given[h], 2)))

    corr_ref[...] = join(solved[0], here(solved[1], 1), half)
    out_ref[...] = join(final[0], here(final[1], 1), half)

    for k in range(steps):
        for q in range(QUARTERS):
            ring_copy(k, q).wait_send()

    @pl.when(row % 2 == 0)
    def _():
        for h in range(2):
            for copy in trace_copies(h)[0]():
                copy.wait_send()

    @pl.when(row == 1)
    def _():
        for h in range(2):
            for copy in trace_copies(h)[1]():
                copy.wait_send()
            for i in range(2):
                stage_copy(h, i).wait_send()

    @pl.when(row == 2)
    def _():
        cross_down().wait_send()

    for j in range(sectors - 1):
        for side in range(2):

            @pl.when(passes_on(side, j))
            def _():
                relay_copy(side, j).wait_send()


def leave_kernel(corr_ref, out_ref, corr_hbm, out_hbm, sems):
    copies = [
        pltpu.make_async_copy(corr_ref, corr_hbm, sems.at[0]),
        pltpu.make_async_copy(out_ref, out_hbm, sems.at[1]),
    ]
    for copy in copies:
        copy.start()
    for copy in copies:
        copy.wait()


def ring_device(residual, block_inverse, cycle_coupling, outlet_flux, inlet_lift, mortar_shift):
    blk, lines = residual.shape[-2:]
    face = outlet_flux.shape[-2]
    sectors = lax.axis_size("sector")
    steps = sectors - 1
    vmem = pl.BlockSpec(memory_space=pltpu.VMEM)
    hbm = pl.BlockSpec(memory_space=pl.ANY)
    dma = pltpu.SemaphoreType.DMA
    corr, out = pl.pallas_call(
        functools.partial(ring_kernel, sectors),
        out_shape=(pltpu.VMEM((blk, lines), F32), pltpu.VMEM((face, lines), F32)),
        in_specs=[hbm] * 6,
        out_specs=(vmem, vmem),
        scratch_shapes=[
            pltpu.SMEM(mortar_shift.shape, jnp.int32),
            pltpu.VMEM((blk, lines), F32),
            pltpu.VMEM((blk, blk), F32),
            pltpu.VMEM((blk, blk), F32),
            pltpu.VMEM((face, blk), F32),
            pltpu.VMEM((face, blk), F32),
            pltpu.VMEM((blk, 3 * blk), BF16),
            pltpu.VMEM((face, 3 * blk), BF16),
            pltpu.VMEM((face, 3 * blk), BF16),
            pltpu.VMEM((blk + face, 3 * face), BF16),
            pltpu.VMEM((face, 3 * face), BF16),
            pltpu.VMEM((face, 3 * face), BF16),
            pltpu.VMEM((blk, lines), F32),
            pltpu.VMEM((face, lines), F32),
            pltpu.VMEM((steps, QUARTERS, blk // QUARTERS, lines), F32),
            pltpu.VMEM((steps, QUARTERS, blk // QUARTERS, lines), F32),
            pltpu.VMEM((2, blk, lines), F32),
            pltpu.VMEM((2, face // 2, lines), F32),
            pltpu.VMEM((2, face, lines), F32),
            pltpu.VMEM((2, face, lines), F32),
            pltpu.VMEM((sectors, face // 2, lines), F32),
            pltpu.VMEM((sectors, face // 2, lines), F32),
            pltpu.VMEM((sectors, face // 2, lines), F32),
            pltpu.VMEM((sectors, face // 2, lines), F32),
            pltpu.VMEM((2 * sectors, face, face), F32),
            pltpu.VMEM((2, 2, face // 2, lines), F32),
            pltpu.VMEM((2, face // 2, lines), F32),
            dma((QUARTERS + 5,)),
            dma((steps, QUARTERS)),
            dma((steps, QUARTERS)),
            dma((2, sectors)),
            dma((2, sectors)),
            dma((2, sectors)),
            dma((1,)),
            dma((2, sectors)),
            dma((sectors,)),
            dma((2, 2)),
            dma((2,)),
        ],
        compiler_params=pltpu.CompilerParams(
            collective_id=0, has_side_effects=True, vmem_limit_bytes=62 * 2**20
        ),
        name="ring",
    )(
        mortar_shift,
        residual.reshape(blk, lines),
        block_inverse.reshape(blk, blk),
        cycle_coupling.reshape(blk, blk),
        outlet_flux.reshape(face, blk),
        jnp.swapaxes(inlet_lift, -1, -2).reshape(face, blk),
    )
    corr, out = pl.pallas_call(
        leave_kernel,
        out_shape=(
            jax.ShapeDtypeStruct((blk, lines), F32),
            jax.ShapeDtypeStruct((face, lines), F32),
        ),
        in_specs=[hbm, hbm],
        out_specs=(hbm, hbm),
        scratch_shapes=[dma((2,))],
        compiler_params=pltpu.CompilerParams(vmem_limit_bytes=2**20),
        name="leave",
    )(corr, out)
    return corr.reshape(residual.shape), out.reshape(outlet_flux.shape[:-1] + (lines,))


def from_behind(block, axis, distance):
    devices = range(lax.axis_size(axis))
    route = [((i - distance) % len(devices), i) for i in devices]
    return lax.ppermute(block, axis, route)


def from_behind_2(value, axis, steps):
    count = lax.axis_size(axis)
    leading, last = (max(0, -steps), min(count, count - steps))
    return lax.ppermute(value, axis, [(source, source + steps) for source in range(leading, last)])


def apply_block(matrix, state):
    return jnp.einsum("ij,bjl->bil", matrix, state, precision=HIGH)


def turn_sectors(trace, offset, levels):
    for level in range(levels):
        moved = from_behind(trace, "sector", 2**level)
        trace = jnp.where(offset // 2**level % 2 == 1, moved, trace)
    return trace


def pass_down(trace):
    return from_behind_2(trace, "row", 1)


def doubling_device(residual, block_inverse, cycle_coupling, outlet_flux, inlet_lift, mortar_shift):
    res_local = residual[0, 0]
    inverse = block_inverse[0, 0]
    coupling = cycle_coupling[0, 0]
    flux = outlet_flux[0, 0]
    lift = inlet_lift[0, 0]
    source = jnp.einsum("bij,bjl->bil", inverse, res_local, precision=HIGH)
    levels = lax.axis_size("sector").bit_length() - 1
    matrix = coupling
    state = source
    for level in range(levels):
        if level + 1 < levels:
            prev_matrix, prev_state = from_behind((matrix, state), "sector", 2**level)
            state = state + apply_block(matrix, prev_state)
            matrix = jnp.dot(matrix, prev_matrix, precision=HIGH)
        else:
            prev_state = from_behind(state, "sector", 2**level)
            state = state + apply_block(matrix, prev_state)
    row_count = lax.axis_size("row")
    row_index = lax.axis_index("row")
    offset = jnp.sum(
        jnp.where(jnp.arange(row_count - 1, dtype=jnp.int32) == row_index - 1, mortar_shift, 0)
    )
    bands = state.shape[0]
    current = state
    band_ids = jnp.arange(bands, dtype=jnp.int32)
    for step in range(1, row_count + bands - 1):
        send_band = jnp.clip(step - 1 - row_index, 0, bands - 1)
        flux_one = lax.dynamic_index_in_dim(flux, send_band, 0, keepdims=False)
        state_one = lax.dynamic_index_in_dim(current, send_band, 0, keepdims=False)
        trace = jnp.dot(flux_one, state_one, precision=HIGH)[None]
        moved = turn_sectors(pass_down(trace), offset, levels)[0]
        band = step - row_index
        band_clip = jnp.clip(band, 0, bands - 1)
        lift_one = lax.dynamic_index_in_dim(lift, band_clip, 0, keepdims=False)
        solved_one = lax.dynamic_index_in_dim(state, band_clip, 0, keepdims=False)
        update = solved_one + jnp.dot(lift_one, moved, precision=HIGH)
        valid = jnp.logical_and(row_index >= 1, jnp.logical_and(band >= 0, band < bands))
        chosen = jnp.logical_and(valid, band_ids == band)[:, None, None]
        current = jnp.where(chosen, update[None], current)
    outlet = jnp.einsum("bfj,bjl->bfl", flux, current, precision=HIGH)
    return (current[None, None], outlet[None, None])


def solution(mesh):
    in_specs = (
        P("row", "sector", "band", None, None),
        P("row", "sector", "band", None, None),
        P("row", "sector", None, None),
        P("row", "sector", "band", None, None),
        P("row", "sector", "band", None, None),
        P(),
    )
    out_specs = (P("row", "sector", "band", None, None), P("row", "sector", "band", None, None))
    short = mesh.shape["sector"] <= RING_LIMIT and mesh.shape["row"] == 4
    on_device = ring_device if short else doubling_device
    return jax.shard_map(
        on_device, mesh=mesh, in_specs=in_specs, out_specs=out_specs, check_vma=False
    )
```

```python
import functools

import jax
import jax.numpy as jnp
from jax import lax
from jax.experimental import pallas as pl
from jax.experimental.pallas import tpu as pltpu
from jax.sharding import PartitionSpec as P

HIGH = lax.Precision.HIGHEST
MESH = pl.DeviceIdType.MESH
F32 = jnp.float32
BF16 = jnp.bfloat16
RING_LIMIT = 8
QUARTERS = 4


def split(value):
    top = value.astype(BF16)
    return top, (value - top.astype(F32)).astype(BF16)


def dot(a, b):
    return jnp.dot(a, b, preferred_element_type=F32)


def times(a_top, a_rest, b):
    b_top, b_rest = split(b)
    width = b.shape[1]
    wide = dot(a_top, jnp.concatenate([b_top, b_rest], axis=1))
    return wide[:, :width] + (wide[:, width:] + dot(a_rest, b_top))


def keep(ref, matrix):
    depth = matrix.shape[1]
    top, rest = split(matrix)
    ref[:, :depth] = top
    ref[:, depth : 2 * depth] = top
    ref[:, 2 * depth :] = rest


def product(kept, b):
    top, rest = split(b)
    return dot(kept[...], jnp.concatenate([top, rest, top], axis=0))


def turn_lanes(value, by):
    by %= value.shape[1]
    return pltpu.roll(value, by, axis=1) if by else value


def pack(value, parts):
    high, width = value.shape[0] // parts, value.shape[1] // parts
    lane = lax.broadcasted_iota(jnp.int32, (high, value.shape[1]), 1)
    out = value[:high]
    for i in range(1, parts):
        block = turn_lanes(value[i * high : (i + 1) * high], i * width)
        out = jnp.where(lane < i * width, out, block)
    return out


def spread(value, parts, at=0):
    width = value.shape[1] // parts
    return jnp.concatenate(
        [turn_lanes(value, (at - i) * width) for i in range(parts)], axis=0
    )


def join(left, right, width):
    lane = lax.broadcasted_iota(jnp.int32, left.shape, 1)
    return jnp.where(lane < width, left, right)


def ring_kernel(
    sectors,
    shift_hbm, res_hbm, inv_hbm, coup_hbm, flux_hbm, lift_hbm,
    corr_ref, out_ref,
    shift_ref, res, inv, coup, flux, lift, coup3, flux3, flow3, end3, other3_a, other3_b,
    source, seen, state, landed, solved, trace, face_trace, final, above_a, above_b, beside_a, beside_b, crosses, stage, given,
    load_sem, send_sem, recv_sem, above_recv, beside_recv, trace_send,
    cross_send, cross_recv, stage_send, given_recv,
):
    row = lax.axis_index("row")
    sector = lax.axis_index("sector")
    above, beside, other3 = (above_a, above_b), (beside_a, beside_b), (other3_a, other3_b)
    lines = res.shape[1]
    quarter, half = lines // QUARTERS, lines // 2
    depth, face = coup.shape[1], flux.shape[0]

    def turn(k):
        return lax.rem(sector + k, sectors)

    def remote(src, dst, send, recv, down, k):
        return pltpu.make_async_remote_copy(
            src_ref=src, dst_ref=dst, send_sem=send, recv_sem=recv,
            device_id={"row": row + down, "sector": turn(k)}, device_id_type=MESH,
        )

    high = inv.shape[0] // QUARTERS
    blocks = [pl.ds(i * high, high) for i in range(QUARTERS)]
    pairs = [
        (res_hbm, res), (coup_hbm, coup), (flux_hbm, flux), (lift_hbm, lift),
        (shift_hbm, shift_ref),
    ]
    pairs[1:1] = [(inv_hbm.at[block], inv.at[block]) for block in blocks]
    loads = [
        pltpu.make_async_copy(src, dst, load_sem.at[i]) for i, (src, dst) in enumerate(pairs)
    ]
    for load in loads:
        load.start()

    barrier = pltpu.get_barrier_semaphore()

    def greet(up, k):
        pl.semaphore_signal(
            barrier, inc=1, device_id={"row": row - up, "sector": turn(k)}, device_id_type=MESH
        )

    greet(0, sectors - 1)

    @pl.when(row == 1)
    def _():
        for k in range(1, sectors - 1):
            greet(0, k)

    @pl.when(row % 2 == 1)
    def _():
        for k in range(sectors):
            greet(1, k)

    @pl.when(row >= 2)
    def _():
        greet(row - 1, 0)

    loads.pop(0).wait()
    for block in blocks:
        loads.pop(0).wait()
        source[block] = times(*split(inv[block]), res[...])

    @pl.when(row % 2 == 0)
    def _():
        pl.semaphore_wait(barrier, sectors + 1)

    @pl.when(row == 1)
    def _():
        pl.semaphore_wait(barrier, sectors + 1)

    @pl.when(row == 3)
    def _():
        pl.semaphore_wait(barrier, 1)

    def cross_copies():
        return (
            lambda: [
                remote(crosses.at[sector], crosses.at[sector], cross_send.at[k], cross_recv.at[sector], 0, k)
                for k in range(1, sectors)
            ],
            lambda: [
                remote(crosses.at[sector], above_cross(sector), cross_send.at[k], cross_recv.at[sector], 1, k)
                for k in range(sectors)
            ],
        )

    def above_cross(k):
        return crosses.at[sectors + k]

    steps = sectors - 1

    def ring_copy(k, q):
        return remote(
            state.at[k, q], landed.at[k, q], send_sem.at[k, q], recv_sem.at[k, q], 0, 1
        )

    for q in range(QUARTERS):
        state[0, q] = pack(turn_lanes(source[...], -q * quarter), QUARTERS)
        ring_copy(0, q).start()

    loads[0].wait()
    keep(coup3, coup[...])
    loads[1].wait()
    loads[2].wait()
    crosses[sector] = times(*split(flux[...]), lift[...].T)

    @pl.when(row == 1)
    def _():
        for copy in cross_copies()[0]():
            copy.start()

    @pl.when(row == 2)
    def _():
        for copy in cross_copies()[1]():
            copy.start()

    loads[3].wait()
    shift = [shift_ref[i] for i in range(3)]

    def back(by):
        return lax.rem(sector + 2 * sectors - by, sectors)

    def ready_flux():
        keep(flux3, flux[...])
        seen[...] = product(flux3, source[...])

    def ready_flow():
        flux_top, flux_rest = split(flux[...])
        coup_top, coup_rest = coup3[:, :depth], coup3[:, 2 * depth :]
        rest = dot(flux_top, coup_rest) + dot(flux_rest, coup_top)
        keep(flow3, dot(flux_top, coup_top) + rest)

    def ready_lift():
        keep(end3, jnp.concatenate([lift[...].T, crosses[sector]], axis=0))

    def ready_other():
        @pl.when(row == 1)
        def _():
            for i in range(1, sectors):
                remote(
                    crosses.at[turn(i)], crosses.at[turn(i)], cross_send.at[i],
                    cross_recv.at[turn(i)], 0, i,
                ).wait_recv()
            keep(other3[0], crosses[back(shift[1])])
            keep(other3[1], crosses[back(shift[1] + shift[2])])

        @pl.when(row == 3)
        def _():
            for i in range(sectors):
                remote(
                    crosses.at[0], above_cross(i), cross_send.at[i], cross_recv.at[i], -1, i
                ).wait_recv()
            keep(other3[0], crosses[sectors + back(shift[2])])

    ready_flux()
    last = QUARTERS - 1
    aside = {(0, last - 1): ready_flow, (0, last): ready_lift, (1, last): ready_other}

    far_first = sorted(range(1, sectors), key=lambda k: abs(2 * k - sectors)) + [0]

    def trace_copies(h):
        return (
            lambda: [
                remote(trace.at[h], above[h].at[sector], trace_send.at[h, k], above_recv.at[h, sector], 1, k)
                for k in far_first
            ],
            lambda: [
                remote(trace.at[h], beside[h].at[sector], trace_send.at[h, k], beside_recv.at[h, sector], 0, k)
                for k in far_first[:-1]
            ],
        )

    for k in range(steps - 1):
        for q in range(QUARTERS):
            ring_copy(k, q).wait_recv()
            came = product(coup3, spread(landed[k, q], QUARTERS))
            state[k + 1, q] = state[0, q] + pack(came, QUARTERS)
            ring_copy(k + 1, q).start()
            if (k, q) in aside:
                aside.pop((k, q))()
    for left in aside.values():
        left()

    def here(value, h):
        return turn_lanes(value, h * half)

    for h in range(2):
        each = range(h * QUARTERS // 2, (h + 1) * QUARTERS // 2)
        came = None
        for at, q in enumerate(each):
            ring_copy(steps - 1, q).wait_recv()
            more = spread(landed[steps - 1, q], QUARTERS, at)
            came = more if came is None else join(came, more, at * quarter)
        face_trace[h] = here(seen[...], h) + product(flow3, came)
        trace[h] = pack(face_trace[h], 2)

        @pl.when(row % 2 == 0)
        def _():
            for copy in trace_copies(h)[0]():
                copy.start()

        @pl.when(row == 1)
        def _():
            for copy in trace_copies(h)[1]():
                copy.start()

        solved[h] = here(source[...], h) + product(coup3, came)

    def wait_above(h):
        for i in range(sectors):
            remote(
                trace.at[h], above[h].at[i], trace_send.at[h, 0], above_recv.at[h, i], -1, i
            ).wait_recv()

    def stage_copy(h, i):
        return remote(
            stage.at[h, i], given.at[h], stage_send.at[h, i], given_recv.at[h], i + 1, 0
        )

    def finish(h, moved):
        both = product(end3, moved)
        solved[h] += both[:depth]
        final[h] = face_trace[h] + both[depth:]

    @pl.when(row == 0)
    def _():
        final[...] = face_trace[...]

    @pl.when(row == 1)
    def _():
        for h in range(2):
            wait_above(h)
            for i in range(1, sectors):
                remote(
                    trace.at[h], beside[h].at[turn(i)], trace_send.at[h, i],
                    beside_recv.at[h, turn(i)], 0, i,
                ).wait_recv()
            beside[h][sector] = trace[h]
            for i, by in ((1, shift[1] + shift[2]), (0, shift[1])):
                moved = above[h][lax.rem(back(by) + sectors - shift[0], sectors)]
                stage[h, i] = beside[h][back(by)] + pack(product(other3[i], spread(moved, 2)), 2)
                stage_copy(h, i).start()
        for h in range(2):
            finish(h, spread(above[h][back(shift[0])], 2))

    @pl.when(row == 2)
    def _():
        for h in range(2):
            stage_copy(h, 0).wait_recv()
            finish(h, spread(given[h], 2))

    @pl.when(row == 3)
    def _():
        for h in range(2):
            wait_above(h)
            moved = spread(above[h][back(shift[2])], 2)
            stage_copy(h, 1).wait_recv()
            finish(h, moved + product(other3[0], spread(given[h], 2)))

    corr_ref[...] = join(solved[0], here(solved[1], 1), half)
    out_ref[...] = join(final[0], here(final[1], 1), half)

    for k in range(steps):
        for q in range(QUARTERS):
            ring_copy(k, q).wait_send()

    @pl.when(row % 2 == 0)
    def _():
        for h in range(2):
            for copy in trace_copies(h)[0]():
                copy.wait_send()

    @pl.when(row == 1)
    def _():
        for copy in cross_copies()[0]():
            copy.wait_send()
        for h in range(2):
            for copy in trace_copies(h)[1]():
                copy.wait_send()
            for i in range(2):
                stage_copy(h, i).wait_send()

    @pl.when(row == 2)
    def _():
        for copy in cross_copies()[1]():
            copy.wait_send()


def leave_kernel(corr_ref, out_ref, corr_hbm, out_hbm, sems):
    copies = [
        pltpu.make_async_copy(corr_ref, corr_hbm, sems.at[0]),
        pltpu.make_async_copy(out_ref, out_hbm, sems.at[1]),
    ]
    for copy in copies:
        copy.start()
    for copy in copies:
        copy.wait()


def ring_device(residual, block_inverse, cycle_coupling, outlet_flux, inlet_lift, mortar_shift):
    blk, lines = residual.shape[-2:]
    face = outlet_flux.shape[-2]
    sectors = lax.axis_size("sector")
    steps = sectors - 1
    vmem = pl.BlockSpec(memory_space=pltpu.VMEM)
    hbm = pl.BlockSpec(memory_space=pl.ANY)
    dma = pltpu.SemaphoreType.DMA
    corr, out = pl.pallas_call(
        functools.partial(ring_kernel, sectors),
        out_shape=(pltpu.VMEM((blk, lines), F32), pltpu.VMEM((face, lines), F32)),
        in_specs=[hbm] * 6,
        out_specs=(vmem, vmem),
        scratch_shapes=[
            pltpu.SMEM(mortar_shift.shape, jnp.int32),
            pltpu.VMEM((blk, lines), F32),
            pltpu.VMEM((blk, blk), F32),
            pltpu.VMEM((blk, blk), F32),
            pltpu.VMEM((face, blk), F32),
            pltpu.VMEM((face, blk), F32),
            pltpu.VMEM((blk, 3 * blk), BF16),
            pltpu.VMEM((face, 3 * blk), BF16),
            pltpu.VMEM((face, 3 * blk), BF16),
            pltpu.VMEM((blk + face, 3 * face), BF16),
            pltpu.VMEM((face, 3 * face), BF16),
            pltpu.VMEM((face, 3 * face), BF16),
            pltpu.VMEM((blk, lines), F32),
            pltpu.VMEM((face, lines), F32),
            pltpu.VMEM((steps, QUARTERS, blk // QUARTERS, lines), F32),
            pltpu.VMEM((steps, QUARTERS, blk // QUARTERS, lines), F32),
            pltpu.VMEM((2, blk, lines), F32),
            pltpu.VMEM((2, face // 2, lines), F32),
            pltpu.VMEM((2, face, lines), F32),
            pltpu.VMEM((2, face, lines), F32),
            pltpu.VMEM((sectors, face // 2, lines), F32),
            pltpu.VMEM((sectors, face // 2, lines), F32),
            pltpu.VMEM((sectors, face // 2, lines), F32),
            pltpu.VMEM((sectors, face // 2, lines), F32),
            pltpu.VMEM((2 * sectors, face, face), F32),
            pltpu.VMEM((2, 2, face // 2, lines), F32),
            pltpu.VMEM((2, face // 2, lines), F32),
            dma((QUARTERS + 5,)),
            dma((steps, QUARTERS)),
            dma((steps, QUARTERS)),
            dma((2, sectors)),
            dma((2, sectors)),
            dma((2, sectors)),
            dma((sectors,)),
            dma((sectors,)),
            dma((2, 2)),
            dma((2,)),
        ],
        compiler_params=pltpu.CompilerParams(
            collective_id=0, has_side_effects=True, vmem_limit_bytes=62 * 2**20
        ),
        name="ring",
    )(
        mortar_shift,
        residual.reshape(blk, lines),
        block_inverse.reshape(blk, blk),
        cycle_coupling.reshape(blk, blk),
        outlet_flux.reshape(face, blk),
        jnp.swapaxes(inlet_lift, -1, -2).reshape(face, blk),
    )
    corr, out = pl.pallas_call(
        leave_kernel,
        out_shape=(
            jax.ShapeDtypeStruct((blk, lines), F32),
            jax.ShapeDtypeStruct((face, lines), F32),
        ),
        in_specs=[hbm, hbm],
        out_specs=(hbm, hbm),
        scratch_shapes=[dma((2,))],
        compiler_params=pltpu.CompilerParams(vmem_limit_bytes=2**20),
        name="leave",
    )(corr, out)
    return corr.reshape(residual.shape), out.reshape(outlet_flux.shape[:-1] + (lines,))


def from_behind(block, axis, distance):
    devices = range(lax.axis_size(axis))
    route = [((i - distance) % len(devices), i) for i in devices]
    return lax.ppermute(block, axis, route)


def from_behind_2(value, axis, steps):
    count = lax.axis_size(axis)
    leading, last = (max(0, -steps), min(count, count - steps))
    return lax.ppermute(value, axis, [(source, source + steps) for source in range(leading, last)])


def apply_block(matrix, state):
    return jnp.einsum("ij,bjl->bil", matrix, state, precision=HIGH)


def turn_sectors(trace, offset, levels):
    for level in range(levels):
        moved = from_behind(trace, "sector", 2**level)
        trace = jnp.where(offset // 2**level % 2 == 1, moved, trace)
    return trace


def pass_down(trace):
    return from_behind_2(trace, "row", 1)


def doubling_device(residual, block_inverse, cycle_coupling, outlet_flux, inlet_lift, mortar_shift):
    res_local = residual[0, 0]
    inverse = block_inverse[0, 0]
    coupling = cycle_coupling[0, 0]
    flux = outlet_flux[0, 0]
    lift = inlet_lift[0, 0]
    source = jnp.einsum("bij,bjl->bil", inverse, res_local, precision=HIGH)
    levels = lax.axis_size("sector").bit_length() - 1
    matrix = coupling
    state = source
    for level in range(levels):
        if level + 1 < levels:
            prev_matrix, prev_state = from_behind((matrix, state), "sector", 2**level)
            state = state + apply_block(matrix, prev_state)
            matrix = jnp.dot(matrix, prev_matrix, precision=HIGH)
        else:
            prev_state = from_behind(state, "sector", 2**level)
            state = state + apply_block(matrix, prev_state)
    row_count = lax.axis_size("row")
    row_index = lax.axis_index("row")
    offset = jnp.sum(
        jnp.where(jnp.arange(row_count - 1, dtype=jnp.int32) == row_index - 1, mortar_shift, 0)
    )
    bands = state.shape[0]
    current = state
    band_ids = jnp.arange(bands, dtype=jnp.int32)
    for step in range(1, row_count + bands - 1):
        send_band = jnp.clip(step - 1 - row_index, 0, bands - 1)
        flux_one = lax.dynamic_index_in_dim(flux, send_band, 0, keepdims=False)
        state_one = lax.dynamic_index_in_dim(current, send_band, 0, keepdims=False)
        trace = jnp.dot(flux_one, state_one, precision=HIGH)[None]
        moved = turn_sectors(pass_down(trace), offset, levels)[0]
        band = step - row_index
        band_clip = jnp.clip(band, 0, bands - 1)
        lift_one = lax.dynamic_index_in_dim(lift, band_clip, 0, keepdims=False)
        solved_one = lax.dynamic_index_in_dim(state, band_clip, 0, keepdims=False)
        update = solved_one + jnp.dot(lift_one, moved, precision=HIGH)
        valid = jnp.logical_and(row_index >= 1, jnp.logical_and(band >= 0, band < bands))
        chosen = jnp.logical_and(valid, band_ids == band)[:, None, None]
        current = jnp.where(chosen, update[None], current)
    outlet = jnp.einsum("bfj,bjl->bfl", flux, current, precision=HIGH)
    return (current[None, None], outlet[None, None])


def solution(mesh):
    in_specs = (
        P("row", "sector", "band", None, None),
        P("row", "sector", "band", None, None),
        P("row", "sector", None, None),
        P("row", "sector", "band", None, None),
        P("row", "sector", "band", None, None),
        P(),
    )
    out_specs = (P("row", "sector", "band", None, None), P("row", "sector", "band", None, None))
    short = mesh.shape["sector"] <= RING_LIMIT and mesh.shape["row"] == 4
    on_device = ring_device if short else doubling_device
    return jax.shard_map(
        on_device, mesh=mesh, in_specs=in_specs, out_specs=out_specs, check_vma=False
    )
```
